128 devices in a mesh: dp: 32 (over z, x_lo, y), tensor: 4 (over x_hi, core).
Axes of the slice: x: 4 (x_hi: 2, x_lo: 2; x = x_hi * 2 + x_lo), y: 4, z: 4, core: 2. Of those that a mesh axis runs over, the one named last changes fastest.
Arguments:
- tokens: bfloat16 [16384, 1152], P(('dp', 'tensor')), may hold values from -6 to 6
- doc_lengths: int32 [16], replicated, may hold values from 1 to 2048, 16384 in all
- norm_gains: float32 [1152, 4], replicated, may hold values from -0.5 to 0.5
- head_gains: float32 [256, 2], replicated, may hold values from -0.5 to 0.5
- q_o: bfloat16 [1152, 2, 1024], P('dp', None, 'tensor'), may hold values from -0.1875 to 0.1875
- kv_weight: bfloat16 [1152, 512], P('dp'), may hold values from -0.1875 to 0.1875
- ffn_weight: bfloat16 [1152, 3, 6912], P('dp', None, 'tensor'), may hold values from -0.1875 to 0.1875
- out_grad: bfloat16 [16384, 1152], P(('dp', 'tensor')), may hold values from -6 to 6
Outputs:
- mixed: bfloat16 [16384, 1152], P(('dp', 'tensor'))
- tokens_grad: bfloat16 [16384, 1152], P(('dp', 'tensor'))
- norm_gains_grad: float32 [1152, 4], P('dp')
- head_gains_grad: float32 [256, 2], P('dp')
- q_o_grad: float32 [1152, 2, 1024], P('dp', None, 'tensor')
- kv_grad: float32 [1152, 512], P('dp')
- ffn_grad: float32 [1152, 3, 6912], P('dp', None, 'tensor')
The draws below stay inside these ranges and needn't reach their ends.
Inputs may be any that keep to these rules, and one draw needn't show every extreme that they name: `doc_lengths`: the lengths sum to 16384; the longest is exactly 2048.
All inputs are finite; a program needn't handle non-finite values.
Results may differ from the reference program's by a relative error of at most 0.033.
Values may be sent and summed in bfloat16 or wider, within the bound.
No kernel may reach another device: no remote copies, remote signals or barrier semaphores. Data moves between devices by JAX's collectives and lax.ppermute only.
A program may use at most 128 MiB of HBM per device.

```python
import math
import jax
import jax.numpy as jnp
import numpy as np
from jax import lax

D = 1152
HEADS = 4
HD = 256
FF = 6912
WINDOW = 512
DOC_MOST = 2048
GRP_TOK = 512
TOKENS = 16384
NDOC = 16


def shard_levels(own_key, shape, split, smallest, largest):
    level = 1.0
    for dim, blocks in split:
        steps = jax.random.uniform(jax.random.fold_in(jax.random.fold_in(own_key, 6), dim), (blocks,), jnp.float32, smallest / len(split), largest / len(split))
        level = level * jnp.repeat(jnp.exp(steps), shape[dim] // blocks).reshape((-1,) + (1,) * (len(shape) - 1 - dim))
    return level


def length_profile(amount, total, most, skew):
    portions = [(1 << 20) // math.isqrt(grade ** skew) + 1 for grade in range(2, amount + 1)]
    surplus, counts = total - most - (amount - 1), [1] * (amount - 1)
    while surplus > 0:
        movable = [i for i in range(amount - 1) if counts[i] < most]
        whole, left = sum([portions[i] for i in movable]), surplus
        for i in movable:
            more = min(most - counts[i], max(1, left * portions[i] // whole), surplus)
            counts[i] = counts[i] + more
            surplus = surplus - more
    return np.array([most] + counts)


def uneven_parts(own_key, number_of, total, most, skew):
    if number_of == 2:
        one = jax.random.randint(own_key, (), max(1, total - most), min(most, total - 1) + 1)
        return jnp.stack([one, total - one])
    sizes = jnp.asarray(length_profile(number_of, total, most, skew), jnp.int32)
    pairs = (number_of - 1) // 2
    source_of, sink = sizes[1:1 + 2 * pairs:2], sizes[2:2 + 2 * pairs:2]
    room = jnp.minimum(source_of - 1, most - sink)
    passed = jax.random.randint(jax.random.fold_in(own_key, 1), (pairs,), 0, 1 << 20) % (room + 1)
    sizes = sizes.at[1:1 + 2 * pairs:2].set(source_of - passed).at[2:2 + 2 * pairs:2].set(sink + passed)
    return sizes[jax.random.permutation(jax.random.fold_in(own_key, 2), number_of)]


def bell_draw(stream_key, dims, width, bound, split=(), held_as=jnp.bfloat16):
    drawn = jax.random.normal(stream_key, dims, jnp.float32) * width
    if len(split) > 0:
        drawn = shard_levels(stream_key, dims, split, -0.22, 0.18) * drawn
    return jnp.clip(drawn, min=-bound, max=bound).astype(held_as)


def setup_inputs(seed: int = 0) -> dict:
    splits = jax.random.split(jax.random.key(seed), 9)
    tokens = bell_draw(splits[0], (TOKENS, D), 1.0, 6.0, ((0, 128),))
    doc_lengths = uneven_parts(splits[1], NDOC, TOKENS, DOC_MOST, 2).astype(jnp.int32)
    norm_gains = jnp.clip(jax.random.uniform(splits[2], (D, 4), jnp.float32, -0.5, 0.5), -0.5, 0.5)
    head_gains = jnp.clip(jax.random.uniform(splits[3], (HD, 2), jnp.float32, -0.5, 0.5), -0.5, 0.5)
    q_o = bell_draw(splits[4], (D, 2, HEADS * HD), D ** -0.5, 0.1875, ((0, 32), (2, 4)))
    kv_weight = bell_draw(splits[5], (D, 2 * HD), D ** -0.5, 0.1875, ((0, 32),))
    ffn_weight = bell_draw(splits[6], (D, 3, FF), D ** -0.5, 0.1875, ((0, 32), (2, 4)))
    out_grad = bell_draw(splits[7], (TOKENS, D), 1.0, 6.0, ((0, 128),))
    return dict(tokens=tokens, doc_lengths=doc_lengths, norm_gains=norm_gains, head_gains=head_gains, q_o=q_o, kv_weight=kv_weight, ffn_weight=ffn_weight, out_grad=out_grad)


epsilon = 1e-06
rope_base = 10000.0
masked_score = -1e+30
highest = lax.Precision.HIGHEST

@jax.custom_vjp
def low(v):
    return lax.optimization_barrier(v.astype(jnp.bfloat16)).astype(jnp.float32)

@jax.custom_vjp
def low_back(v):
    return v

def low_keep(v):
    return (low(v), None)

def low_pass(kept, grad):
    return (grad,)

def back_keep(v):
    return (v, None)

def back_low(kept, grad):
    return (low(grad),)
low.defvjp(low_keep, low_pass)
low_back.defvjp(back_keep, back_low)

def rms_scale(values, gains):
    mean_square = lax.optimization_barrier(jnp.mean(values * values, axis=-1, keepdims=True))
    return values * lax.rsqrt(mean_square + epsilon) * (1.0 + gains)

def rotate(values, cosine, sine_table):
    half_dim = values.shape[-1] // 2
    front = values[..., :half_dim]
    back_half = values[..., half_dim:]
    return jnp.concatenate([front * cosine - back_half * sine_table, back_half * cosine + front * sine_table], axis=-1)

def rope_tables(position, head_dim):
    half_dim = head_dim // 2
    exponent = jnp.arange(half_dim).astype(jnp.float32) * (-2.0 / head_dim)
    frequency = jnp.power(jnp.float32(rope_base), exponent)
    angle = position.astype(jnp.float32)[:, None] * frequency[None, :]
    return (jnp.cos(angle), jnp.sin(angle))

def document_of(doc_lengths, index):
    ends = jnp.cumsum(doc_lengths).astype(jnp.int32)
    starts = (ends - doc_lengths).astype(jnp.int32)
    doc_number = lax.optimization_barrier(jnp.sum((ends[None, :] <= index[:, None]).astype(jnp.int32), axis=1)).astype(jnp.int32)
    owner = doc_number[:, None] == jnp.arange(doc_lengths.shape[0], dtype=jnp.int32)[None, :]
    position = (index - lax.optimization_barrier(jnp.sum(jnp.where(owner, starts[None, :], 0), axis=1))).astype(jnp.int32)
    return (doc_number, position)

def geglu(gate_in, up_in):
    return jax.nn.gelu(gate_in, approximate=True) * up_in

def forward(inputs, norm_gains, head_gains, q_o, kv_weight, ffn_weight, doc_number, cosine, sine_table):
    head_dim = head_gains.shape[0]
    score_scale = head_dim ** (-0.5)
    count = inputs.shape[0]
    heads = q_o.shape[2] // head_dim
    blocks = count // GRP_TOK
    normed = low(rms_scale(inputs, norm_gains[:, 0]))
    queries = low_back(jnp.dot(normed, q_o[:, 0, :], precision=highest))
    key_val = jnp.dot(normed, kv_weight, precision=highest)
    key_raw = low_back(key_val[:, :head_dim])
    value_low = low_back(low(key_val[:, head_dim:]))
    queries = queries.reshape(count, heads, head_dim)
    query_rot = low(rotate(rms_scale(queries, head_gains[:, 0]), cosine[:, None, :], sine_table[:, None, :]))
    key_rot = low(rotate(rms_scale(key_raw, head_gains[:, 1]), cosine, sine_table))
    index = jnp.arange(count, dtype=jnp.int32)

    def with_earlier(array, filler):
        earlier = jnp.concatenate([filler, array[:-GRP_TOK]], axis=0)
        tail_shape = array.shape[1:]
        return jnp.concatenate([earlier.reshape((blocks, GRP_TOK) + tail_shape), array.reshape((blocks, GRP_TOK) + tail_shape)], axis=1)
    key_blocks = with_earlier(key_rot, jnp.zeros((GRP_TOK, head_dim), key_rot.dtype))
    value_blocks = with_earlier(value_low, jnp.zeros((GRP_TOK, head_dim), value_low.dtype))
    key_docs = with_earlier(doc_number, jnp.full((GRP_TOK,), -1, jnp.int32))
    key_places = with_earlier(index, (index[:GRP_TOK] - GRP_TOK).astype(jnp.int32))

    def attend(block_in):
        query_blk, key_blk, value_blk, query_doc, key_doc, query_at, key_at = block_in
        scores = jnp.einsum('qhd,kd->hqk', query_blk, key_blk, precision=highest) * score_scale
        scores = low_back(scores)
        distance = query_at[:, None] - key_at[None, :]
        allowed = (query_doc[:, None] == key_doc[None, :]) & (distance >= 0) & (distance < WINDOW)
        scores = jnp.where(allowed[None, :, :], scores, masked_score)
        top_score = lax.optimization_barrier(jnp.max(scores, axis=2, keepdims=True))
        weights = jnp.exp(scores - top_score)
        probs = low(weights / lax.optimization_barrier(jnp.sum(weights, axis=2, keepdims=True)))
        return jnp.einsum('hqk,kd->qhd', probs, value_blk, precision=highest)
    attended = lax.map(jax.checkpoint(attend), (query_rot.reshape(blocks, GRP_TOK, heads, head_dim), key_blocks, value_blocks, doc_number.reshape(blocks, GRP_TOK), key_docs, index.reshape(blocks, GRP_TOK), key_places))
    attended = low_back(low(attended.reshape(count, heads * head_dim)))

    def finish(pair):
        inputs_blk, attn_blk = pair
        attn_out = low_back(jnp.dot(attn_blk, q_o[:, 1, :].T, precision=highest))
        resid = inputs_blk + rms_scale(attn_out, norm_gains[:, 1])
        ffn_in = low(rms_scale(resid, norm_gains[:, 2]))
        gate_val = low_back(jnp.dot(ffn_in, ffn_weight[:, 0, :], precision=highest))
        up_val = low_back(jnp.dot(ffn_in, ffn_weight[:, 1, :], precision=highest))
        hidden = low(geglu(gate_val, up_val))
        ffn_out = low_back(jnp.dot(hidden, ffn_weight[:, 2, :].T, precision=highest))
        return resid + rms_scale(ffn_out, norm_gains[:, 3])
    mixed = lax.map(jax.checkpoint(finish), (inputs.reshape(blocks, GRP_TOK, D), attended.reshape(blocks, GRP_TOK, heads * head_dim)))
    return mixed.reshape(count, D)

def reference(tokens, doc_lengths, norm_gains, head_gains, q_o, kv_weight, ffn_weight, out_grad):
    index = jnp.arange(TOKENS, dtype=jnp.int32)
    doc_number, position = document_of(doc_lengths, index)
    cosine, sine_table = rope_tables(position, HD)

    def layer(inputs, norm_in, head_in, qo_in, kv_in, ffn_in):
        return forward(inputs, norm_in, head_in, qo_in, kv_in, ffn_in, doc_number, cosine, sine_table)
    mixed, pull = jax.vjp(layer, tokens.astype(jnp.float32), norm_gains.astype(jnp.float32), head_gains.astype(jnp.float32), q_o.astype(jnp.float32), kv_weight.astype(jnp.float32), ffn_weight.astype(jnp.float32))
    grads = pull(out_grad.astype(jnp.float32))
    return (mixed.astype(jnp.bfloat16), grads[0].astype(jnp.bfloat16), grads[1], grads[2], grads[3], grads[4], grads[5])
```

```python
import jax
import jax.numpy as jnp
import numpy as np
from jax import lax
from jax.sharding import Mesh
from jax.sharding import PartitionSpec as P

WINDOW = 512
NZ, NXL, NY, NXH, NC = 4, 2, 4, 2, 2
ALL = ("z", "xl", "y", "xh", "c")
ZY = ("z", "y")
BLOCKS = NZ * NXL * NY * NXH * NC

epsilon = 1e-06
rope_base = 10000.0
masked_score = -1e30
bf16 = jnp.bfloat16
f32 = jnp.float32


def rms_scale(values, gains):
    mean_square = jnp.mean(values * values, axis=-1, keepdims=True)
    return values * lax.rsqrt(mean_square + epsilon) * (1.0 + gains)


def norm_back(values, gains, upstream):
    inverse = lax.rsqrt(jnp.mean(values * values, axis=-1, keepdims=True) + epsilon)
    normed = values * inverse
    scaled = upstream * (1.0 + gains)
    grad_values = inverse * (scaled - normed * jnp.mean(scaled * normed, axis=-1, keepdims=True))
    return (grad_values, upstream * normed)


def rotate(values, cosine, sine_table):
    half_dim = values.shape[-1] // 2
    front = values[..., :half_dim]
    back_half = values[..., half_dim:]
    return jnp.concatenate(
        [front * cosine - back_half * sine_table, back_half * cosine + front * sine_table], axis=-1
    )


def rope_tables(position, head_dim):
    half_dim = head_dim // 2
    exponent = jnp.arange(half_dim).astype(f32) * (-2.0 / head_dim)
    frequency = jnp.power(f32(rope_base), exponent)
    angle = position.astype(f32)[:, None] * frequency[None, :]
    return (jnp.cos(angle), jnp.sin(angle))


def document_of(doc_lengths, index):
    ends = jnp.cumsum(doc_lengths)
    starts = ends - doc_lengths
    doc_number = jnp.sum((ends[None, :] <= index[:, None]).astype(jnp.int32), axis=1)
    owner = doc_number[:, None] == jnp.arange(doc_lengths.shape[0], dtype=jnp.int32)[None, :]
    position = index - jnp.sum(jnp.where(owner, starts[None, :], 0), axis=1)
    return (doc_number, position)


def geglu(gate_in, up_in):
    return jax.nn.gelu(gate_in, approximate=True) * up_in


def matmul(left, right):
    return jnp.dot(left, right, preferred_element_type=f32)


def matmul_nt(left, right):
    return lax.dot_general(left, right, (((1,), (1,)), ((), ())), preferred_element_type=f32)


def matmul_tn(left, right):
    return lax.dot_general(left, right, (((0,), (0,)), ((), ())), preferred_element_type=f32)


def swap(array, axis):
    return lax.ppermute(array, axis, [(0, 1), (1, 0)])


def swap_both(array):
    return lax.ppermute(array, ("xl", "xh"), [(0, 3), (1, 2), (2, 1), (3, 0)])


def shifted(array, by):
    return lax.ppermute(
        array, ALL, [(i, i + by) for i in range(BLOCKS) if 0 <= i + by < BLOCKS]
    )


def group_rows(own):
    pair = jnp.concatenate([own, swap(own, "xh")], axis=0)
    return jnp.concatenate([pair, swap(pair, "c")], axis=0)


def group_sum(part):
    half = part.shape[0] // 2
    mine = part[:half].astype(f32) + swap(part[half:], "c").astype(f32)
    mine = mine.astype(bf16)
    own = half // 2
    return mine[:own].astype(f32) + swap(mine[own:], "xh").astype(f32)


def body(tokens, doc_lengths, norm_gains, head_gains, q_o, kv_weight, ffn_weight, out_grad):
    rows = tokens.shape[0]
    dim = tokens.shape[1]
    head_dim = head_gains.shape[0]
    score_scale = head_dim ** (-0.5)
    xl = lax.axis_index("xl")
    c = lax.axis_index("c")
    dp_rows = q_o.shape[0]
    ff = ffn_weight.shape[2]
    ff_pad = -ff % 256
    wide = ff + ff_pad

    ffn_own = jnp.pad(ffn_weight, ((0, 0), (0, 0), (0, ff_pad))).reshape(dp_rows, 3 * wide)
    ffn_pair = jnp.concatenate([ffn_own, swap(ffn_own, "xl")], axis=0)
    kv_half = lax.dynamic_slice_in_dim(kv_weight, c * head_dim, head_dim, 1)
    q_own, o_own = q_o[:, 0, :], q_o[:, 1, :]
    small = jnp.concatenate([q_own, kv_half, o_own], axis=1)
    from_xl, from_xh, from_both = swap(small, "xl"), swap(small, "xh"), swap_both(small)

    def beside(first, second):
        return jnp.concatenate(
            [
                first[:, :head_dim],
                second[:, :head_dim],
                first[:, head_dim : 2 * head_dim],
                first[:, 2 * head_dim :],
                second[:, 2 * head_dim :],
            ],
            axis=1,
        )

    attn_pair = jnp.concatenate([beside(small, from_xh), beside(from_xl, from_both)], axis=0)
    attn_a = lax.all_to_all(
        jnp.broadcast_to(attn_pair[None], (NZ * NY, *attn_pair.shape)), ZY, 0, 0, tiled=True
    ).reshape(dim, -1)
    attn_b = swap(attn_a, "c")
    ffn_full = lax.all_gather(ffn_pair, ZY, axis=0, tiled=True)

    new = jnp.arange(dim, dtype=jnp.int32)
    z_of, y_of = new // (dp_rows * NXL * NY), (new // (dp_rows * NXL)) % NY
    xl_of = jnp.bitwise_xor((new // dp_rows) % NXL, xl)
    old = ((z_of * NXL + xl_of) * NY + y_of) * dp_rows + new % dp_rows
    order = (jnp.arange(dim, dtype=jnp.int32)[:, None] == old[None, :]).astype(bf16)

    def reordered(array):
        tail = array.shape[1:]
        cut = array.reshape(NZ, NXL, NY, dp_rows, *tail)
        first = jnp.where(xl == 0, cut[:, 0], cut[:, 1])
        second = jnp.where(xl == 0, cut[:, 1], cut[:, 0])
        return jnp.stack([first, second], axis=2).reshape(dim, *tail)

    gains = reordered(norm_gains)
    inputs = matmul(tokens, order)
    upstream = matmul(out_grad, order)

    block = ((lax.axis_index("z") * NXL + xl) * NY + lax.axis_index("y")) * NXH * NC
    block = block + lax.axis_index("xh") * NC + c
    back = WINDOW // rows
    key_index = (block - back) * rows + jnp.arange((back + 1) * rows, dtype=jnp.int32)
    key_doc, key_position = document_of(doc_lengths, key_index)
    key_doc = jnp.where(key_index < 0, -1, key_doc)
    query_index = key_index[back * rows :]
    query_doc = key_doc[back * rows :]
    cosine, sine_table = rope_tables(key_position[back * rows :], head_dim)
    distance = query_index[:, None] - key_index[None, :]
    allowed = (query_doc[:, None] == key_doc[None, :]) & (distance >= 0) & (distance < WINDOW)

    normed = rms_scale(inputs, gains[:, 0]).astype(bf16)
    qkv_a = matmul(normed, attn_a[:, : 3 * head_dim])
    qkv_b = matmul(normed, attn_b[:, : 3 * head_dim])
    query_raw = jnp.stack(
        [
            qkv_a[:, :head_dim],
            qkv_a[:, head_dim : 2 * head_dim],
            qkv_b[:, :head_dim],
            qkv_b[:, head_dim : 2 * head_dim],
        ],
        axis=0,
    )
    kv_a, kv_b = qkv_a[:, 2 * head_dim :], qkv_b[:, 2 * head_dim :]
    key_raw = jnp.where(c == 0, kv_a, kv_b)
    value_low = jnp.where(c == 0, kv_b, kv_a).astype(bf16)
    key_rot = rotate(rms_scale(key_raw, head_gains[:, 1]), cosine, sine_table).astype(bf16)
    packed = jnp.concatenate([key_rot, value_low], axis=1)
    both = jnp.concatenate([shifted(packed, by) for by in range(back, 0, -1)] + [packed], axis=0)
    key_all, value_all = both[:, :head_dim], both[:, head_dim:]
    query_rot = rotate(rms_scale(query_raw, head_gains[:, 0]), cosine, sine_table).astype(bf16)
    heads = query_raw.shape[0]
    query_flat = query_rot.reshape(heads * rows, head_dim)
    scores = matmul_nt(query_flat, key_all).reshape(heads, rows, -1) * score_scale
    scores = jnp.where(allowed[None], scores, masked_score)
    top_score = jnp.max(scores, axis=2, keepdims=True)
    weights = jnp.exp(scores - top_score)
    total = jnp.sum(weights, axis=2, keepdims=True)
    probs_full = (weights / total).reshape(heads * rows, -1)
    probs = probs_full.astype(bf16)
    attended = matmul(probs, value_all).astype(bf16).reshape(heads, rows, head_dim)
    attended_a = jnp.concatenate([attended[0], attended[1]], axis=1)
    attended_b = jnp.concatenate([attended[2], attended[3]], axis=1)
    out_a, out_b = attn_a[:, 3 * head_dim :], attn_b[:, 3 * head_dim :]
    attn_out = matmul_nt(attended_a, out_a) + matmul_nt(attended_b, out_b)
    resid = inputs + rms_scale(attn_out, gains[:, 1])

    ffn_in = group_rows(rms_scale(resid, gains[:, 2]).astype(bf16))
    w_gate, w_up, w_down = ffn_full[:, :wide], ffn_full[:, wide : 2 * wide], ffn_full[:, 2 * wide :]
    gate_up = matmul(ffn_in, ffn_full[:, : 2 * wide])
    gate_val, up_val = gate_up[:, :wide], gate_up[:, wide:]
    hidden = geglu(gate_val, up_val).astype(bf16)
    ffn_out = group_sum(matmul_nt(hidden, w_down).astype(bf16))
    mixed = (resid + rms_scale(ffn_out, gains[:, 3])).astype(bf16)
    grad_ffn_out, gain_three = norm_back(ffn_out, gains[:, 3], upstream)
    grad_ffn = group_rows(grad_ffn_out.astype(bf16))
    grad_hidden = matmul(grad_ffn, w_down)
    unused_value, pull = jax.vjp(geglu, gate_val, up_val)
    grad_gate, grad_up = pull(grad_hidden)
    grad_gate_up = jnp.concatenate([grad_gate.astype(bf16), grad_up.astype(bf16)], axis=1)
    grad_ffn_in = group_sum(matmul_nt(grad_gate_up, ffn_full[:, : 2 * wide]).astype(bf16))
    grad_w = jnp.concatenate(
        [matmul_tn(ffn_in, grad_gate_up).astype(bf16), matmul_tn(grad_ffn, hidden).astype(bf16)],
        axis=1,
    )
    ffn_rows = lax.psum_scatter(grad_w, ZY, scatter_dimension=0, tiled=True)

    grad_from_ffn, gain_two = norm_back(resid, gains[:, 2], grad_ffn_in)
    grad_resid = upstream + grad_from_ffn
    grad_attn_out, gain_one = norm_back(attn_out, gains[:, 1], grad_resid)
    grad_attn = grad_attn_out.astype(bf16)

    att_grad_a = matmul(grad_attn, out_a).astype(bf16)
    att_grad_b = matmul(grad_attn, out_b).astype(bf16)
    grad_attended = jnp.concatenate(
        [
            att_grad_a[:, :head_dim],
            att_grad_a[:, head_dim:],
            att_grad_b[:, :head_dim],
            att_grad_b[:, head_dim:],
        ],
        axis=0,
    )
    grad_value_all = matmul_tn(probs, grad_attended)
    grad_probs = matmul_nt(grad_attended, value_all)
    inner = jnp.sum(probs_full * grad_probs, axis=1, keepdims=True)
    grad_scores = (probs_full * (grad_probs - inner)).astype(bf16)
    grad_query_rot = (matmul(grad_scores, key_all) * score_scale).reshape(heads, rows, head_dim)
    grad_key_all = matmul_tn(grad_scores, query_flat) * score_scale
    grad_query_norm = rotate(grad_query_rot, cosine, -sine_table)
    grad_query_raw, gain_query = norm_back(query_raw, head_gains[:, 0], grad_query_norm)
    grad_query = grad_query_raw.astype(bf16)
    key_grads = jnp.concatenate([grad_key_all, grad_value_all], axis=1)
    own_grads = key_grads[back * rows :]
    key_low = key_grads[: back * rows].astype(bf16)
    for by in range(1, back + 1):
        part = key_low[(back - by) * rows : (back - by + 1) * rows]
        own_grads = own_grads + shifted(part, -by).astype(f32)
    grad_key_norm = rotate(own_grads[:, :head_dim], cosine, -sine_table)
    grad_key_raw, gain_key = norm_back(key_raw, head_gains[:, 1], grad_key_norm)
    grad_key = grad_key_raw.astype(bf16)
    grad_value = own_grads[:, head_dim:].astype(bf16)
    grad_kv_a = jnp.where(c == 0, grad_key, grad_value)
    grad_kv_b = jnp.where(c == 0, grad_value, grad_key)
    grad_qkv_a = jnp.concatenate([grad_query[0], grad_query[1], grad_kv_a], axis=1)
    grad_qkv_b = jnp.concatenate([grad_query[2], grad_query[3], grad_kv_b], axis=1)
    grad_normed = matmul_nt(grad_qkv_a, attn_a[:, : 3 * head_dim]) + matmul_nt(
        grad_qkv_b, attn_b[:, : 3 * head_dim]
    )
    grad_from_norm, gain_zero = norm_back(inputs, gains[:, 0], grad_normed)
    tokens_grad = (grad_resid + grad_from_norm).astype(bf16)

    norm_part = jnp.stack(
        [jnp.sum(g, axis=0) for g in (gain_zero, gain_one, gain_two, gain_three)], axis=1
    )
    head_part = jnp.stack([jnp.sum(gain_query, axis=(0, 1)), jnp.sum(gain_key, axis=0)], axis=1)
    head_cut = head_part.reshape(NZ, NXL, NY, -1)
    head_cut = jnp.stack(
        [
            jnp.where(xl == 0, head_cut[:, 0], head_cut[:, 1]),
            jnp.where(xl == 0, head_cut[:, 1], head_cut[:, 0]),
        ],
        axis=2,
    )
    per_dp = head_cut.shape[-1]
    head_column = jnp.pad(head_cut, ((0, 0), (0, 0), (0, 0), (0, dp_rows - per_dp)))
    gain_cols = jnp.concatenate([norm_part, head_column.reshape(dim, 1)], axis=1)
    n_gain = gain_cols.shape[1]
    gain_cols = jnp.pad(gain_cols, ((0, 0), (0, 128 - n_gain))).astype(bf16)

    def weight_part(grad_qkv, att):
        return jnp.concatenate(
            [
                matmul_tn(normed, grad_qkv).astype(bf16),
                matmul_tn(grad_attn, att).astype(bf16),
                gain_cols,
            ],
            axis=1,
        )

    mine = weight_part(grad_qkv_a, attended_a).astype(f32)
    other = swap(weight_part(grad_qkv_b, attended_b), "c").astype(f32)
    part = (mine + other).astype(bf16)
    arrived = lax.all_to_all(part, ZY, 0, 0, tiled=True).reshape(NZ * NY, NXL * dp_rows, -1)
    zy_sum = jnp.sum(arrived.astype(f32), axis=0).astype(bf16)

    def columns(array, which):
        k = which * head_dim
        return jnp.concatenate(
            [
                array[:, k : k + head_dim],
                array[:, 2 * head_dim : 3 * head_dim],
                array[:, 3 * head_dim + k : 4 * head_dim + k],
                array[:, 5 * head_dim :],
            ],
            axis=1,
        )

    near, far = zy_sum[:dp_rows], zy_sum[dp_rows:]
    x_sum = (
        columns(near, 0).astype(f32)
        + swap(columns(far, 0), "xl").astype(f32)
        + swap(columns(near, 1), "xh").astype(f32)
        + swap_both(columns(far, 1)).astype(f32)
    )
    qo_share = jnp.stack(
        [x_sum[:, :head_dim], x_sum[:, 2 * head_dim : 3 * head_dim]], axis=1
    )
    kv_mine = x_sum[:, head_dim : 2 * head_dim]
    kv_other = swap(kv_mine.astype(bf16), "c").astype(f32)
    kv_mine = kv_mine.astype(bf16).astype(f32)
    kv_total = jnp.concatenate(
        [jnp.where(c == 0, kv_mine, kv_other), jnp.where(c == 0, kv_other, kv_mine)], axis=1
    )
    norm_total = x_sum[:, 3 * head_dim : 3 * head_dim + 4]
    head_total = x_sum[:per_dp, 3 * head_dim + 4].reshape(-1, 2)

    ffn_share = ffn_rows[:dp_rows].astype(f32) + swap(ffn_rows[dp_rows:], "xl").astype(f32)
    ffn_share = ffn_share.reshape(dp_rows, 3, wide)[:, :, :ff]

    def restored(array):
        return matmul_nt(array, order).astype(bf16)

    return (
        restored(mixed),
        restored(tokens_grad),
        norm_total,
        head_total,
        qo_share,
        kv_total,
        ffn_share,
    )


def solution(mesh):
    fine = Mesh(np.asarray(mesh.devices).reshape(NZ, NXL, NY, NXH, NC), ALL)
    dp, tensor = ("z", "xl", "y"), ("xh", "c")
    return jax.shard_map(
        body,
        mesh=fine,
        in_specs=(
            P(ALL, None),
            P(),
            P(),
            P(),
            P(dp, None, tensor),
            P(dp, None),
            P(dp, None, tensor),
            P(ALL, None),
        ),
        out_specs=(
            P(ALL, None),
            P(ALL, None),
            P(dp, None),
            P(dp, None),
            P(dp, None, tensor),
            P(dp, None),
            P(dp, None, tensor),
        ),
        check_vma=False,
    )
```

```python
import jax
import jax.numpy as jnp
import numpy as np
from jax import lax
from jax.sharding import Mesh
from jax.sharding import PartitionSpec as P

WINDOW = 512
NZ, NXL, NY, NXH, NC = 4, 2, 4, 2, 2
ALL = ("z", "xl", "y", "xh", "c")
ZY = ("z", "y")
BLOCKS = NZ * NXL * NY * NXH * NC

epsilon = 1e-06
rope_base = 10000.0
masked_score = -1e30
bf16 = jnp.bfloat16
f32 = jnp.float32


def rms_scale(values, gains):
    mean_square = jnp.mean(values * values, axis=-1, keepdims=True)
    return values * lax.rsqrt(mean_square + epsilon) * (1.0 + gains)


def norm_back(values, gains, upstream):
    inverse = lax.rsqrt(jnp.mean(values * values, axis=-1, keepdims=True) + epsilon)
    normed = values * inverse
    scaled = upstream * (1.0 + gains)
    grad_values = inverse * (scaled - normed * jnp.mean(scaled * normed, axis=-1, keepdims=True))
    return (grad_values, upstream * normed)


def rotate(values, cosine, sine_table):
    half_dim = values.shape[-1] // 2
    front = values[..., :half_dim]
    back_half = values[..., half_dim:]
    return jnp.concatenate(
        [front * cosine - back_half * sine_table, back_half * cosine + front * sine_table], axis=-1
    )


def rope_tables(position, head_dim):
    half_dim = head_dim // 2
    exponent = jnp.arange(half_dim).astype(f32) * (-2.0 / head_dim)
    frequency = jnp.power(f32(rope_base), exponent)
    angle = position.astype(f32)[:, None] * frequency[None, :]
    return (jnp.cos(angle), jnp.sin(angle))


def document_of(doc_lengths, index):
    ends = jnp.cumsum(doc_lengths)
    starts = ends - doc_lengths
    doc_number = jnp.sum((ends[None, :] <= index[:, None]).astype(jnp.int32), axis=1)
    owner = doc_number[:, None] == jnp.arange(doc_lengths.shape[0], dtype=jnp.int32)[None, :]
    position = index - jnp.sum(jnp.where(owner, starts[None, :], 0), axis=1)
    return (doc_number, position)


def geglu(gate_in, up_in):
    return jax.nn.gelu(gate_in, approximate=True) * up_in


def matmul(left, right):
    return jnp.dot(left, right, preferred_element_type=f32)


def matmul_nt(left, right):
    return lax.dot_general(left, right, (((1,), (1,)), ((), ())), preferred_element_type=f32)


def matmul_tn(left, right):
    return lax.dot_general(left, right, (((0,), (0,)), ((), ())), preferred_element_type=f32)


def swap(array, axis):
    return lax.ppermute(array, axis, [(0, 1), (1, 0)])


def swap_both(array):
    return lax.ppermute(array, ("xl", "xh"), [(0, 3), (1, 2), (2, 1), (3, 0)])


def shifted(array, by):
    return lax.ppermute(
        array, ALL, [(i, i + by) for i in range(BLOCKS) if 0 <= i + by < BLOCKS]
    )


def moved(array, axis, by):
    peers = lax.axis_size(axis)
    return lax.ppermute(array, axis, [(i, (i + by) % peers) for i in range(peers)])


def gathered(own, axis, dim):
    peers, me = lax.axis_size(axis), lax.axis_index(axis)
    own = jnp.expand_dims(own, dim)
    shape = own.shape[:dim] + (peers,) + own.shape[dim + 1 :]
    pieces = [moved(own, axis, by) for by in (1, 3, 2)]
    whole = jnp.broadcast_to(own, shape)
    for by, piece in zip((1, 3, 2), pieces):
        whole = lax.dynamic_update_slice_in_dim(whole, piece, (me - by) % peers, dim)
    return whole


def summed(whole, axis, dim):
    peers, me = lax.axis_size(axis), lax.axis_index(axis)

    def block(by):
        return lax.dynamic_index_in_dim(whole, (me + by) % peers, dim, keepdims=False)

    arrived = [moved(block(by).astype(bf16), axis, by) for by in (1, 3, 2)]
    return sum((a.astype(f32) for a in arrived), block(0).astype(f32))


def group_rows(own):
    pair = jnp.concatenate([own, swap(own, "xh")], axis=0)
    return jnp.concatenate([pair, swap(pair, "c")], axis=0)


def group_sum(part):
    half = part.shape[0] // 2
    mine = part[:half].astype(f32) + swap(part[half:], "c").astype(f32)
    mine = mine.astype(bf16)
    own = half // 2
    return mine[:own].astype(f32) + swap(mine[own:], "xh").astype(f32)


def body(tokens, doc_lengths, norm_gains, head_gains, q_o, kv_weight, ffn_weight, out_grad):
    rows = tokens.shape[0]
    dim = tokens.shape[1]
    head_dim = head_gains.shape[0]
    score_scale = head_dim ** (-0.5)
    xl = lax.axis_index("xl")
    c = lax.axis_index("c")
    dp_rows = q_o.shape[0]
    ff = ffn_weight.shape[2]
    ff_pad = -ff % 256
    wide = ff + ff_pad

    kv_half = lax.dynamic_slice_in_dim(kv_weight, c * head_dim, head_dim, 1)
    q_own, o_own = q_o[:, 0, :], q_o[:, 1, :]
    small = jnp.concatenate([q_own, kv_half, o_own], axis=1)
    small, ffn_weight = lax.optimization_barrier((small, ffn_weight))
    from_xl, from_xh, from_both = swap(small, "xl"), swap(small, "xh"), swap_both(small)
    ffn_own = jnp.pad(ffn_weight, ((0, 0), (0, 0), (0, ff_pad))).reshape(dp_rows, 3 * wide)
    ffn_pair = jnp.concatenate([ffn_own, swap(ffn_own, "xl")], axis=0)

    def beside(first, second):
        return jnp.concatenate(
            [
                first[:, :head_dim],
                second[:, :head_dim],
                first[:, head_dim : 2 * head_dim],
                first[:, 2 * head_dim :],
                second[:, 2 * head_dim :],
            ],
            axis=1,
        )

    attn_pair = jnp.concatenate([beside(small, from_xh), beside(from_xl, from_both)], axis=0)
    part = attn_pair.shape[1] // 2
    left = gathered(gathered(attn_pair[:, :part], "y", 0), "z", 0).reshape(dim, part)
    right = gathered(gathered(attn_pair[:, part:], "z", 0), "y", 1).reshape(dim, part)
    attn_a = jnp.concatenate([left, right], axis=1)
    attn_b = jnp.concatenate([swap(left, "c"), swap(right, "c")], axis=1)
    ffn_full = lax.all_gather(ffn_pair, ZY, axis=0, tiled=True)

    new = jnp.arange(dim, dtype=jnp.int32)
    z_of, y_of = new // (dp_rows * NXL * NY), (new // (dp_rows * NXL)) % NY
    xl_of = jnp.bitwise_xor((new // dp_rows) % NXL, xl)
    old = ((z_of * NXL + xl_of) * NY + y_of) * dp_rows + new % dp_rows
    order = (jnp.arange(dim, dtype=jnp.int32)[:, None] == old[None, :]).astype(bf16)

    def reordered(array):
        tail = array.shape[1:]
        cut = array.reshape(NZ, NXL, NY, dp_rows, *tail)
        first = jnp.where(xl == 0, cut[:, 0], cut[:, 1])
        second = jnp.where(xl == 0, cut[:, 1], cut[:, 0])
        return jnp.stack([first, second], axis=2).reshape(dim, *tail)

    gains = reordered(norm_gains)
    inputs = matmul(tokens, order)
    upstream = matmul(out_grad, order)

    block = ((lax.axis_index("z") * NXL + xl) * NY + lax.axis_index("y")) * NXH * NC
    block = block + lax.axis_index("xh") * NC + c
    back = WINDOW // rows
    key_index = (block - back) * rows + jnp.arange((back + 1) * rows, dtype=jnp.int32)
    key_doc, key_position = document_of(doc_lengths, key_index)
    key_doc = jnp.where(key_index < 0, -1, key_doc)
    query_index = key_index[back * rows :]
    query_doc = key_doc[back * rows :]
    cosine, sine_table = rope_tables(key_position[back * rows :], head_dim)
    distance = query_index[:, None] - key_index[None, :]
    allowed = (query_doc[:, None] == key_doc[None, :]) & (distance >= 0) & (distance < WINDOW)

    normed = rms_scale(inputs, gains[:, 0]).astype(bf16)
    qkv_a = matmul(normed, attn_a[:, : 3 * head_dim])
    qkv_b = matmul(normed, attn_b[:, : 3 * head_dim])
    query_raw = jnp.stack(
        [
            qkv_a[:, :head_dim],
            qkv_a[:, head_dim : 2 * head_dim],
            qkv_b[:, :head_dim],
            qkv_b[:, head_dim : 2 * head_dim],
        ],
        axis=0,
    )
    kv_a, kv_b = qkv_a[:, 2 * head_dim :], qkv_b[:, 2 * head_dim :]
    key_raw = jnp.where(c == 0, kv_a, kv_b)
    value_low = jnp.where(c == 0, kv_b, kv_a).astype(bf16)
    key_rot = rotate(rms_scale(key_raw, head_gains[:, 1]), cosine, sine_table).astype(bf16)
    packed = jnp.concatenate([key_rot, value_low], axis=1)
    both = jnp.concatenate([shifted(packed, by) for by in range(back, 0, -1)] + [packed], axis=0)
    key_all, value_all = both[:, :head_dim], both[:, head_dim:]
    query_rot = rotate(rms_scale(query_raw, head_gains[:, 0]), cosine, sine_table).astype(bf16)
    heads = query_raw.shape[0]
    query_flat = query_rot.reshape(heads * rows, head_dim)
    scores = matmul_nt(query_flat, key_all).reshape(heads, rows, -1) * score_scale
    scores = jnp.where(allowed[None], scores, masked_score)
    top_score = jnp.max(scores, axis=2, keepdims=True)
    weights = jnp.exp(scores - top_score)
    total = jnp.sum(weights, axis=2, keepdims=True)
    probs_full = (weights / total).reshape(heads * rows, -1)
    probs = probs_full.astype(bf16)
    attended = matmul(probs, value_all).astype(bf16).reshape(heads, rows, head_dim)
    attended_a = jnp.concatenate([attended[0], attended[1]], axis=1)
    attended_b = jnp.concatenate([attended[2], attended[3]], axis=1)
    out_a, out_b = attn_a[:, 3 * head_dim :], attn_b[:, 3 * head_dim :]
    attn_out = matmul_nt(attended_a, out_a) + matmul_nt(attended_b, out_b)
    resid = inputs + rms_scale(attn_out, gains[:, 1])

    ffn_in = group_rows(rms_scale(resid, gains[:, 2]).astype(bf16))
    w_gate, w_up, w_down = ffn_full[:, :wide], ffn_full[:, wide : 2 * wide], ffn_full[:, 2 * wide :]
    gate_up = matmul(ffn_in, ffn_full[:, : 2 * wide])
    gate_val, up_val = gate_up[:, :wide], gate_up[:, wide:]
    hidden = geglu(gate_val, up_val).astype(bf16)
    ffn_out = group_sum(matmul_nt(hidden, w_down).astype(bf16))
    mixed = (resid + rms_scale(ffn_out, gains[:, 3])).astype(bf16)
    grad_ffn_out, gain_three = norm_back(ffn_out, gains[:, 3], upstream)
    grad_ffn = group_rows(grad_ffn_out.astype(bf16))
    grad_hidden = matmul(grad_ffn, w_down)
    unused_value, pull = jax.vjp(geglu, gate_val, up_val)
    grad_gate, grad_up = pull(grad_hidden)
    grad_gate_up = jnp.concatenate([grad_gate.astype(bf16), grad_up.astype(bf16)], axis=1)
    grad_ffn_in = group_sum(matmul_nt(grad_gate_up, ffn_full[:, : 2 * wide]).astype(bf16))
    grad_w = jnp.concatenate(
        [matmul_tn(ffn_in, grad_gate_up).astype(bf16), matmul_tn(grad_ffn, hidden).astype(bf16)],
        axis=1,
    )
    ffn_rows = lax.psum_scatter(
        grad_w.reshape(NZ * NY, NXL * dp_rows, 3 * wide), ZY, scatter_dimension=0, tiled=False
    )

    grad_from_ffn, gain_two = norm_back(resid, gains[:, 2], grad_ffn_in)
    grad_resid = upstream + grad_from_ffn
    grad_attn_out, gain_one = norm_back(attn_out, gains[:, 1], grad_resid)
    grad_attn = grad_attn_out.astype(bf16)

    att_grad_a = matmul(grad_attn, out_a).astype(bf16)
    att_grad_b = matmul(grad_attn, out_b).astype(bf16)
    grad_attended = jnp.concatenate(
        [
            att_grad_a[:, :head_dim],
            att_grad_a[:, head_dim:],
            att_grad_b[:, :head_dim],
            att_grad_b[:, head_dim:],
        ],
        axis=0,
    )
    grad_value_all = matmul_tn(probs, grad_attended)
    grad_probs = matmul_nt(grad_attended, value_all)
    inner = jnp.sum(probs_full * grad_probs, axis=1, keepdims=True)
    grad_scores = (probs_full * (grad_probs - inner)).astype(bf16)
    grad_query_rot = (matmul(grad_scores, key_all) * score_scale).reshape(heads, rows, head_dim)
    grad_key_all = matmul_tn(grad_scores, query_flat) * score_scale
    grad_query_norm = rotate(grad_query_rot, cosine, -sine_table)
    grad_query_raw, gain_query = norm_back(query_raw, head_gains[:, 0], grad_query_norm)
    grad_query = grad_query_raw.astype(bf16)
    key_grads = jnp.concatenate([grad_key_all, grad_value_all], axis=1)
    own_grads = key_grads[back * rows :]
    key_low = key_grads[: back * rows].astype(bf16)
    for by in range(1, back + 1):
        part = key_low[(back - by) * rows : (back - by + 1) * rows]
        own_grads = own_grads + shifted(part, -by).astype(f32)
    grad_key_norm = rotate(own_grads[:, :head_dim], cosine, -sine_table)
    grad_key_raw, gain_key = norm_back(key_raw, head_gains[:, 1], grad_key_norm)
    grad_key = grad_key_raw.astype(bf16)
    grad_value = own_grads[:, head_dim:].astype(bf16)
    grad_kv_a = jnp.where(c == 0, grad_key, grad_value)
    grad_kv_b = jnp.where(c == 0, grad_value, grad_key)
    grad_qkv_a = jnp.concatenate([grad_query[0], grad_query[1], grad_kv_a], axis=1)
    grad_qkv_b = jnp.concatenate([grad_query[2], grad_query[3], grad_kv_b], axis=1)
    grad_normed = matmul_nt(grad_qkv_a, attn_a[:, : 3 * head_dim]) + matmul_nt(
        grad_qkv_b, attn_b[:, : 3 * head_dim]
    )
    grad_from_norm, gain_zero = norm_back(inputs, gains[:, 0], grad_normed)
    tokens_grad = (grad_resid + grad_from_norm).astype(bf16)

    norm_part = jnp.stack(
        [jnp.sum(g, axis=0) for g in (gain_zero, gain_one, gain_two, gain_three)], axis=1
    )
    head_part = jnp.stack([jnp.sum(gain_query, axis=(0, 1)), jnp.sum(gain_key, axis=0)], axis=1)
    head_cut = head_part.reshape(NZ, NXL, NY, -1)
    head_cut = jnp.stack(
        [
            jnp.where(xl == 0, head_cut[:, 0], head_cut[:, 1]),
            jnp.where(xl == 0, head_cut[:, 1], head_cut[:, 0]),
        ],
        axis=2,
    )
    per_dp = head_cut.shape[-1]
    head_column = jnp.pad(head_cut, ((0, 0), (0, 0), (0, 0), (0, dp_rows - per_dp)))
    gain_cols = jnp.concatenate([norm_part, head_column.reshape(dim, 1)], axis=1)
    n_gain = gain_cols.shape[1]
    gain_cols = jnp.pad(gain_cols, ((0, 0), (0, 128 - n_gain))).astype(bf16)

    def weight_part(grad_qkv, att):
        return jnp.concatenate(
            [
                matmul_tn(normed, grad_qkv).astype(bf16),
                matmul_tn(grad_attn, att).astype(bf16),
                gain_cols,
            ],
            axis=1,
        )

    other = swap(weight_part(grad_qkv_b, attended_b), "c").astype(f32)
    mine = weight_part(grad_qkv_a, attended_a).astype(f32)
    chip = (mine + other).astype(bf16).reshape(NZ, NY, NXL * dp_rows, -1)
    zy_left = summed(summed(chip[..., :768], "y", 1), "z", 0)
    zy_right = summed(summed(chip[..., 768:], "z", 0), "y", 0)
    zy_sum = jnp.concatenate([zy_left, zy_right], axis=-1).astype(bf16)

    def columns(array, which):
        k = which * head_dim
        return jnp.concatenate(
            [
                array[:, k : k + head_dim],
                array[:, 2 * head_dim : 3 * head_dim],
                array[:, 3 * head_dim + k : 4 * head_dim + k],
                array[:, 5 * head_dim :],
            ],
            axis=1,
        )

    near, far = zy_sum[:dp_rows], zy_sum[dp_rows:]
    x_sum = (
        columns(near, 0).astype(f32)
        + swap(columns(far, 0), "xl").astype(f32)
        + swap(columns(near, 1), "xh").astype(f32)
        + swap_both(columns(far, 1)).astype(f32)
    )
    qo_share = jnp.stack(
        [x_sum[:, :head_dim], x_sum[:, 2 * head_dim : 3 * head_dim]], axis=1
    )
    kv_mine = x_sum[:, head_dim : 2 * head_dim]
    kv_other = swap(kv_mine.astype(bf16), "c").astype(f32)
    kv_mine = kv_mine.astype(bf16).astype(f32)
    kv_total = jnp.concatenate(
        [jnp.where(c == 0, kv_mine, kv_other), jnp.where(c == 0, kv_other, kv_mine)], axis=1
    )
    norm_total = x_sum[:, 3 * head_dim : 3 * head_dim + 4]
    head_total = x_sum[:per_dp, 3 * head_dim + 4].reshape(-1, 2)

    ffn_share = ffn_rows[:dp_rows].astype(f32) + swap(ffn_rows[dp_rows:], "xl").astype(f32)
    ffn_share = ffn_share.reshape(dp_rows, 3, wide)[:, :, :ff]

    def restored(array):
        return matmul_nt(array, order).astype(bf16)

    return (
        restored(mixed),
        restored(tokens_grad),
        norm_total,
        head_total,
        qo_share,
        kv_total,
        ffn_share,
    )


def solution(mesh):
    fine = Mesh(np.asarray(mesh.devices).reshape(NZ, NXL, NY, NXH, NC), ALL)
    dp, tensor = ("z", "xl", "y"), ("xh", "c")
    return jax.shard_map(
        body,
        mesh=fine,
        in_specs=(
            P(ALL, None),
            P(),
            P(),
            P(),
            P(dp, None, tensor),
            P(dp, None),
            P(dp, None, tensor),
            P(ALL, None),
        ),
        out_specs=(
            P(ALL, None),
            P(ALL, None),
            P(dp, None),
            P(dp, None),
            P(dp, None, tensor),
            P(dp, None),
            P(dp, None, tensor),
        ),
        check_vma=False,
    )
```

```python
import jax
import jax.numpy as jnp
import numpy as np
from jax import lax
from jax.sharding import Mesh
from jax.sharding import PartitionSpec as P

WINDOW = 512
NZ, NXL, NY, NXH, NC = 4, 2, 4, 2, 2
ALL = ("z", "xl", "y", "xh", "c")
ZY = ("z", "y")
BLOCKS = NZ * NXL * NY * NXH * NC

epsilon = 1e-06
rope_base = 10000.0
masked_score = -1e30
bf16 = jnp.bfloat16
f32 = jnp.float32


def rms_scale(values, gains):
    mean_square = jnp.mean(values * values, axis=-1, keepdims=True)
    return values * lax.rsqrt(mean_square + epsilon) * (1.0 + gains)


def norm_back(values, gains, upstream):
    inverse = lax.rsqrt(jnp.mean(values * values, axis=-1, keepdims=True) + epsilon)
    normed = values * inverse
    scaled = upstream * (1.0 + gains)
    grad_values = inverse * (scaled - normed * jnp.mean(scaled * normed, axis=-1, keepdims=True))
    return (grad_values, upstream * normed)


def rotate(values, cosine, sine_table):
    half_dim = values.shape[-1] // 2
    front = values[..., :half_dim]
    back_half = values[..., half_dim:]
    return jnp.concatenate(
        [front * cosine - back_half * sine_table, back_half * cosine + front * sine_table], axis=-1
    )


def rope_tables(position, head_dim):
    half_dim = head_dim // 2
    exponent = jnp.arange(half_dim).astype(f32) * (-2.0 / head_dim)
    frequency = jnp.power(f32(rope_base), exponent)
    angle = position.astype(f32)[:, None] * frequency[None, :]
    return (jnp.cos(angle), jnp.sin(angle))


def document_of(doc_lengths, index):
    ends = jnp.cumsum(doc_lengths)
    starts = ends - doc_lengths
    doc_number = jnp.sum((ends[None, :] <= index[:, None]).astype(jnp.int32), axis=1)
    owner = doc_number[:, None] == jnp.arange(doc_lengths.shape[0], dtype=jnp.int32)[None, :]
    position = index - jnp.sum(jnp.where(owner, starts[None, :], 0), axis=1)
    return (doc_number, position)


def geglu(gate_in, up_in):
    return jax.nn.gelu(gate_in, approximate=True) * up_in


def matmul(left, right):
    return jnp.dot(left, right, preferred_element_type=f32)


def matmul_nt(left, right):
    return lax.dot_general(left, right, (((1,), (1,)), ((), ())), preferred_element_type=f32)


def matmul_tn(left, right):
    return lax.dot_general(left, right, (((0,), (0,)), ((), ())), preferred_element_type=f32)


def swap(array, axis):
    return lax.ppermute(array, axis, [(0, 1), (1, 0)])


def swap_both(array):
    return lax.ppermute(array, ("xl", "xh"), [(0, 3), (1, 2), (2, 1), (3, 0)])


def shifted(array, by):
    return lax.ppermute(
        array, ALL, [(i, i + by) for i in range(BLOCKS) if 0 <= i + by < BLOCKS]
    )


def moved(array, axis, by):
    peers = lax.axis_size(axis)
    return lax.ppermute(array, axis, [(i, (i + by) % peers) for i in range(peers)])


def gathered(own, axis, dim):
    peers, me = lax.axis_size(axis), lax.axis_index(axis)
    own = jnp.expand_dims(own, dim)
    shape = own.shape[:dim] + (peers,) + own.shape[dim + 1 :]
    pieces = [moved(own, axis, by) for by in (1, 3, 2)]
    whole = jnp.broadcast_to(own, shape)
    for by, piece in zip((1, 3, 2), pieces):
        whole = lax.dynamic_update_slice_in_dim(whole, piece, (me - by) % peers, dim)
    return whole


def summed(terms, axis, dim):
    peers, me = lax.axis_size(axis), lax.axis_index(axis)

    def block(by):
        return sum(
            lax.dynamic_index_in_dim(t, (me + by) % peers, dim, keepdims=False).astype(f32)
            for t in terms
        )

    arrived = [moved(block(by).astype(bf16), axis, by) for by in (1, 3, 2)]
    return sum((a.astype(f32) for a in arrived), block(0))


def group_rows(own):
    pair = jnp.concatenate([own, swap(own, "xh")], axis=0)
    return jnp.concatenate([pair, swap(pair, "c")], axis=0)


def group_sum(part):
    half = part.shape[0] // 2
    mine = part[:half].astype(f32) + swap(part[half:], "c").astype(f32)
    mine = mine.astype(bf16)
    own = half // 2
    return mine[:own].astype(f32) + swap(mine[own:], "xh").astype(f32)


def body(tokens, doc_lengths, norm_gains, head_gains, q_o, kv_weight, ffn_weight, out_grad):
    rows = tokens.shape[0]
    dim = tokens.shape[1]
    head_dim = head_gains.shape[0]
    score_scale = head_dim ** (-0.5)
    xl = lax.axis_index("xl")
    c = lax.axis_index("c")
    dp_rows = q_o.shape[0]
    ff = ffn_weight.shape[2]
    ff_pad = -ff % 256
    wide = ff + ff_pad

    kv_half = lax.dynamic_slice_in_dim(kv_weight, c * head_dim, head_dim, 1)
    small = jnp.concatenate([q_o[:, 0, :], kv_half, q_o[:, 1, :]], axis=1)
    ffn_own = jnp.pad(ffn_weight, ((0, 0), (0, 0), (0, ff_pad))).reshape(dp_rows, 3 * wide)
    from_xl, from_xh, from_both, ffn_other = lax.optimization_barrier(
        (swap(small, "xl"), swap(small, "xh"), swap_both(small), swap(ffn_own, "xl"))
    )
    ffn_pair = jnp.concatenate([ffn_own, ffn_other], axis=0)
    qkv_cols = 2 * head_dim

    def qkv_beside(first, second):
        return jnp.concatenate(
            [first[:, :head_dim], second[:, :head_dim], first[:, head_dim:qkv_cols]], axis=1
        )

    def out_beside(first, second):
        return jnp.concatenate([first[:, qkv_cols:], second[:, qkv_cols:]], axis=1)

    qkv_pair = jnp.concatenate(
        [qkv_beside(small, from_xh), qkv_beside(from_xl, from_both)], axis=0
    )
    out_pair = jnp.concatenate(
        [out_beside(small, from_xh), out_beside(from_xl, from_both)], axis=0
    )
    w_qkv_a = gathered(gathered(qkv_pair, "y", 0), "z", 0).reshape(dim, -1)
    out_a = gathered(gathered(out_pair, "z", 0), "y", 1).reshape(dim, -1)
    w_qkv_b = swap(w_qkv_a, "c")
    out_b = swap(out_a, "c")
    ffn_full = lax.all_gather(ffn_pair, ZY, axis=0, tiled=True)

    new = jnp.arange(dim, dtype=jnp.int32)
    z_of, y_of = new // (dp_rows * NXL * NY), (new // (dp_rows * NXL)) % NY
    xl_of = jnp.bitwise_xor((new // dp_rows) % NXL, xl)
    old = ((z_of * NXL + xl_of) * NY + y_of) * dp_rows + new % dp_rows
    order = (jnp.arange(dim, dtype=jnp.int32)[:, None] == old[None, :]).astype(bf16)

    def reordered(array):
        tail = array.shape[1:]
        cut = array.reshape(NZ, NXL, NY, dp_rows, *tail)
        first = jnp.where(xl == 0, cut[:, 0], cut[:, 1])
        second = jnp.where(xl == 0, cut[:, 1], cut[:, 0])
        return jnp.stack([first, second], axis=2).reshape(dim, *tail)

    gains = reordered(norm_gains)
    inputs = matmul(tokens, order)
    upstream = matmul(out_grad, order)

    block = ((lax.axis_index("z") * NXL + xl) * NY + lax.axis_index("y")) * NXH * NC
    block = block + lax.axis_index("xh") * NC + c
    back = WINDOW // rows
    key_index = (block - back) * rows + jnp.arange((back + 1) * rows, dtype=jnp.int32)
    key_doc, key_position = document_of(doc_lengths, key_index)
    key_doc = jnp.where(key_index < 0, -1, key_doc)
    query_index = key_index[back * rows :]
    query_doc = key_doc[back * rows :]
    cosine, sine_table = rope_tables(key_position[back * rows :], head_dim)
    distance = query_index[:, None] - key_index[None, :]
    allowed = (query_doc[:, None] == key_doc[None, :]) & (distance >= 0) & (distance < WINDOW)

    normed = rms_scale(inputs, gains[:, 0]).astype(bf16)
    qkv_a = matmul(normed, w_qkv_a)
    qkv_b = matmul(normed, w_qkv_b)
    query_raw = jnp.stack(
        [
            qkv_a[:, :head_dim],
            qkv_a[:, head_dim : 2 * head_dim],
            qkv_b[:, :head_dim],
            qkv_b[:, head_dim : 2 * head_dim],
        ],
        axis=0,
    )
    kv_a, kv_b = qkv_a[:, 2 * head_dim :], qkv_b[:, 2 * head_dim :]
    key_raw = jnp.where(c == 0, kv_a, kv_b)
    value_low = jnp.where(c == 0, kv_b, kv_a).astype(bf16)
    key_rot = rotate(rms_scale(key_raw, head_gains[:, 1]), cosine, sine_table).astype(bf16)
    packed = jnp.concatenate([key_rot, value_low], axis=1)
    both = jnp.concatenate([shifted(packed, by) for by in range(back, 0, -1)] + [packed], axis=0)
    key_all, value_all = both[:, :head_dim], both[:, head_dim:]
    query_rot = rotate(rms_scale(query_raw, head_gains[:, 0]), cosine, sine_table).astype(bf16)
    heads = query_raw.shape[0]
    query_flat = query_rot.reshape(heads * rows, head_dim)
    scores = matmul_nt(query_flat, key_all).reshape(heads, rows, -1) * score_scale
    scores = jnp.where(allowed[None], scores, masked_score)
    top_score = jnp.max(scores, axis=2, keepdims=True)
    weights = jnp.exp(scores - top_score)
    total = jnp.sum(weights, axis=2, keepdims=True)
    probs_full = (weights / total).reshape(heads * rows, -1)
    probs = probs_full.astype(bf16)
    attended = matmul(probs, value_all).astype(bf16).reshape(heads, rows, head_dim)
    attended_a = jnp.concatenate([attended[0], attended[1]], axis=1)
    attended_b = jnp.concatenate([attended[2], attended[3]], axis=1)
    attn_out = matmul_nt(attended_a, out_a) + matmul_nt(attended_b, out_b)
    resid = inputs + rms_scale(attn_out, gains[:, 1])

    ffn_in = group_rows(rms_scale(resid, gains[:, 2]).astype(bf16))
    w_gate, w_up, w_down = ffn_full[:, :wide], ffn_full[:, wide : 2 * wide], ffn_full[:, 2 * wide :]
    gate_up = matmul(ffn_in, ffn_full[:, : 2 * wide])
    gate_val, up_val = gate_up[:, :wide], gate_up[:, wide:]
    hidden = geglu(gate_val, up_val).astype(bf16)
    ffn_out = group_sum(matmul_nt(hidden, w_down).astype(bf16))
    mixed = (resid + rms_scale(ffn_out, gains[:, 3])).astype(bf16)
    grad_ffn_out, gain_three = norm_back(ffn_out, gains[:, 3], upstream)
    grad_ffn = group_rows(grad_ffn_out.astype(bf16))
    grad_hidden = matmul(grad_ffn, w_down)
    unused_value, pull = jax.vjp(geglu, gate_val, up_val)
    grad_gate, grad_up = pull(grad_hidden)
    grad_gate_up = jnp.concatenate([grad_gate.astype(bf16), grad_up.astype(bf16)], axis=1)
    grad_ffn_in = group_sum(matmul_nt(grad_gate_up, ffn_full[:, : 2 * wide]).astype(bf16))
    grad_w = jnp.concatenate(
        [matmul_tn(ffn_in, grad_gate_up).astype(bf16), matmul_tn(grad_ffn, hidden).astype(bf16)],
        axis=1,
    )
    ffn_rows = lax.psum_scatter(
        grad_w.reshape(NZ * NY, NXL * dp_rows, 3 * wide), ZY, scatter_dimension=0, tiled=False
    )
    ffn_rows = lax.optimization_barrier(ffn_rows)

    grad_from_ffn, gain_two = norm_back(resid, gains[:, 2], grad_ffn_in)
    grad_resid = upstream + grad_from_ffn
    grad_attn_out, gain_one = norm_back(attn_out, gains[:, 1], grad_resid)
    grad_attn = grad_attn_out.astype(bf16)

    def cut(array):
        return array.reshape(NZ, NY, NXL * dp_rows, -1)

    out_other = swap(matmul_tn(grad_attn, attended_b).astype(bf16), "c")
    out_mine = matmul_tn(grad_attn, attended_a).astype(bf16)
    out_z = summed([cut(out_mine), cut(out_other)], "z", 0)
    out_zy = summed([out_z], "y", 0).astype(bf16)

    def from_x(near_own, far_own, near_peer, far_peer):
        return (
            near_own.astype(f32)
            + swap(far_own, "xl").astype(f32)
            + swap(near_peer, "xh").astype(f32)
            + swap_both(far_peer).astype(f32)
        )

    out_share = from_x(
        out_zy[:dp_rows, :head_dim],
        out_zy[dp_rows:, :head_dim],
        out_zy[:dp_rows, head_dim:],
        out_zy[dp_rows:, head_dim:],
    )

    att_grad_a = matmul(grad_attn, out_a).astype(bf16)
    att_grad_b = matmul(grad_attn, out_b).astype(bf16)
    grad_attended = jnp.concatenate(
        [
            att_grad_a[:, :head_dim],
            att_grad_a[:, head_dim:],
            att_grad_b[:, :head_dim],
            att_grad_b[:, head_dim:],
        ],
        axis=0,
    )
    grad_value_all = matmul_tn(probs, grad_attended)
    grad_probs = matmul_nt(grad_attended, value_all)
    inner = jnp.sum(probs_full * grad_probs, axis=1, keepdims=True)
    grad_scores = (probs_full * (grad_probs - inner)).astype(bf16)
    grad_query_rot = (matmul(grad_scores, key_all) * score_scale).reshape(heads, rows, head_dim)
    grad_key_all = matmul_tn(grad_scores, query_flat) * score_scale
    grad_query_norm = rotate(grad_query_rot, cosine, -sine_table)
    grad_query_raw, gain_query = norm_back(query_raw, head_gains[:, 0], grad_query_norm)
    grad_query = grad_query_raw.astype(bf16)
    key_grads = jnp.concatenate([grad_key_all, grad_value_all], axis=1)
    own_grads = key_grads[back * rows :]
    key_low = key_grads[: back * rows].astype(bf16)
    for by in range(1, back + 1):
        part = key_low[(back - by) * rows : (back - by + 1) * rows]
        own_grads = own_grads + shifted(part, -by).astype(f32)
    grad_key_norm = rotate(own_grads[:, :head_dim], cosine, -sine_table)
    grad_key_raw, gain_key = norm_back(key_raw, head_gains[:, 1], grad_key_norm)
    grad_key = grad_key_raw.astype(bf16)
    grad_value = own_grads[:, head_dim:].astype(bf16)
    grad_kv_a = jnp.where(c == 0, grad_key, grad_value)
    grad_kv_b = jnp.where(c == 0, grad_value, grad_key)
    grad_qkv_a = jnp.concatenate([grad_query[0], grad_query[1], grad_kv_a], axis=1)
    grad_qkv_b = jnp.concatenate([grad_query[2], grad_query[3], grad_kv_b], axis=1)
    grad_normed = matmul_nt(grad_qkv_a, w_qkv_a) + matmul_nt(grad_qkv_b, w_qkv_b)
    grad_from_norm, gain_zero = norm_back(inputs, gains[:, 0], grad_normed)
    tokens_grad = (grad_resid + grad_from_norm).astype(bf16)

    norm_part = jnp.stack(
        [jnp.sum(g, axis=0) for g in (gain_zero, gain_one, gain_two, gain_three)], axis=1
    )
    head_part = jnp.stack([jnp.sum(gain_query, axis=(0, 1)), jnp.sum(gain_key, axis=0)], axis=1)
    head_cut = head_part.reshape(NZ, NXL, NY, -1)
    head_cut = jnp.stack(
        [
            jnp.where(xl == 0, head_cut[:, 0], head_cut[:, 1]),
            jnp.where(xl == 0, head_cut[:, 1], head_cut[:, 0]),
        ],
        axis=2,
    )
    per_dp = head_cut.shape[-1]
    head_column = jnp.pad(head_cut, ((0, 0), (0, 0), (0, 0), (0, dp_rows - per_dp)))
    gain_cols = jnp.concatenate([norm_part, head_column.reshape(dim, 1)], axis=1)
    n_gain = gain_cols.shape[1]
    gain_cols = jnp.pad(gain_cols, ((0, 0), (0, 128 - n_gain))).astype(bf16)

    qkv_other = swap(matmul_tn(normed, grad_qkv_b).astype(bf16), "c")
    gain_other = swap(gain_cols, "c")
    qkv_mine = matmul_tn(normed, grad_qkv_a).astype(bf16)
    whole_mine = jnp.concatenate([qkv_mine, gain_cols], axis=1)
    whole_other = jnp.concatenate([qkv_other, gain_other], axis=1)
    qkv_y = summed([cut(whole_mine), cut(whole_other)], "y", 1)
    qkv_zy = summed([qkv_y], "z", 0).astype(bf16)

    def columns(array, which):
        k = which * head_dim
        return jnp.concatenate([array[:, k : k + head_dim], array[:, 2 * head_dim :]], axis=1)

    near, far = qkv_zy[:dp_rows], qkv_zy[dp_rows:]
    x_sum = from_x(columns(near, 0), columns(far, 0), columns(near, 1), columns(far, 1))
    qo_share = jnp.stack([x_sum[:, :head_dim], out_share], axis=1)
    kv_mine = x_sum[:, head_dim : 2 * head_dim]
    kv_other = swap(kv_mine.astype(bf16), "c").astype(f32)
    kv_mine = kv_mine.astype(bf16).astype(f32)
    kv_total = jnp.concatenate(
        [jnp.where(c == 0, kv_mine, kv_other), jnp.where(c == 0, kv_other, kv_mine)], axis=1
    )
    norm_total = x_sum[:, 2 * head_dim : 2 * head_dim + 4]
    head_total = x_sum[:per_dp, 2 * head_dim + 4].reshape(-1, 2)

    ffn_share = ffn_rows[:dp_rows].astype(f32) + swap(ffn_rows[dp_rows:], "xl").astype(f32)
    ffn_share = ffn_share.reshape(dp_rows, 3, wide)[:, :, :ff]

    def restored(array):
        return matmul_nt(array, order).astype(bf16)

    return (
        restored(mixed),
        restored(tokens_grad),
        norm_total,
        head_total,
        qo_share,
        kv_total,
        ffn_share,
    )


def solution(mesh):
    fine = Mesh(np.asarray(mesh.devices).reshape(NZ, NXL, NY, NXH, NC), ALL)
    dp, tensor = ("z", "xl", "y"), ("xh", "c")
    return jax.shard_map(
        body,
        mesh=fine,
        in_specs=(
            P(ALL, None),
            P(),
            P(),
            P(),
            P(dp, None, tensor),
            P(dp, None),
            P(dp, None, tensor),
            P(ALL, None),
        ),
        out_specs=(
            P(ALL, None),
            P(ALL, None),
            P(dp, None),
            P(dp, None),
            P(dp, None, tensor),
            P(dp, None),
            P(dp, None, tensor),
        ),
        check_vma=False,
    )
```

```python
import jax
import jax.numpy as jnp
import numpy as np
from jax import lax
from jax.sharding import Mesh
from jax.sharding import PartitionSpec as P

WINDOW = 512
NZ, NXL, NY, NXH, NC = 4, 2, 4, 2, 2
ALL = ("z", "xl", "y", "xh", "c")
ZY = ("z", "y")
BLOCKS = NZ * NXL * NY * NXH * NC

epsilon = 1e-06
rope_base = 10000.0
masked_score = -1e30
bf16 = jnp.bfloat16
f32 = jnp.float32


def rms_scale(values, gains):
    mean_square = jnp.mean(values * values, axis=-1, keepdims=True)
    return values * lax.rsqrt(mean_square + epsilon) * (1.0 + gains)


def norm_back(values, gains, upstream):
    inverse = lax.rsqrt(jnp.mean(values * values, axis=-1, keepdims=True) + epsilon)
    normed = values * inverse
    scaled = upstream * (1.0 + gains)
    grad_values = inverse * (scaled - normed * jnp.mean(scaled * normed, axis=-1, keepdims=True))
    return (grad_values, upstream * normed)


def rotate(values, cosine, sine_table):
    half_dim = values.shape[-1] // 2
    front = values[..., :half_dim]
    back_half = values[..., half_dim:]
    return jnp.concatenate(
        [front * cosine - back_half * sine_table, back_half * cosine + front * sine_table], axis=-1
    )


def rope_tables(position, head_dim):
    half_dim = head_dim // 2
    exponent = jnp.arange(half_dim).astype(f32) * (-2.0 / head_dim)
    frequency = jnp.power(f32(rope_base), exponent)
    angle = position.astype(f32)[:, None] * frequency[None, :]
    return (jnp.cos(angle), jnp.sin(angle))


def document_of(doc_lengths, index):
    ends = jnp.cumsum(doc_lengths)
    starts = ends - doc_lengths
    doc_number = jnp.sum((ends[None, :] <= index[:, None]).astype(jnp.int32), axis=1)
    owner = doc_number[:, None] == jnp.arange(doc_lengths.shape[0], dtype=jnp.int32)[None, :]
    position = index - jnp.sum(jnp.where(owner, starts[None, :], 0), axis=1)
    return (doc_number, position)


def geglu(gate_in, up_in):
    return jax.nn.gelu(gate_in, approximate=True) * up_in


def matmul(left, right):
    return jnp.dot(left, right, preferred_element_type=f32)


def matmul_nt(left, right):
    return lax.dot_general(left, right, (((1,), (1,)), ((), ())), preferred_element_type=f32)


def matmul_tn(left, right):
    return lax.dot_general(left, right, (((0,), (0,)), ((), ())), preferred_element_type=f32)


def swap(array, axis):
    return lax.ppermute(array, axis, [(0, 1), (1, 0)])


def swap_both(array):
    return lax.ppermute(array, ("xl", "xh"), [(0, 3), (1, 2), (2, 1), (3, 0)])


def shifted(array, by):
    return lax.ppermute(
        array, ALL, [(i, i + by) for i in range(BLOCKS) if 0 <= i + by < BLOCKS]
    )


def gathered(own):
    blocks = jnp.broadcast_to(own[None], (NZ * NY, *own.shape))
    return lax.all_to_all(blocks, ZY, 0, 0, tiled=True).reshape(-1, own.shape[1])


def summed(terms):
    whole = sum(t.astype(f32) for t in terms).astype(bf16)
    arrived = lax.all_to_all(whole, ZY, 0, 0, tiled=True)
    return jnp.sum(arrived.reshape(NZ * NY, -1, whole.shape[1]).astype(f32), axis=0)


def group_rows(own):
    pair = jnp.concatenate([own, swap(own, "xh")], axis=0)
    return jnp.concatenate([pair, swap(pair, "c")], axis=0)


def group_sum(part):
    half = part.shape[0] // 2
    mine = part[:half].astype(f32) + swap(part[half:], "c").astype(f32)
    mine = mine.astype(bf16)
    own = half // 2
    return mine[:own].astype(f32) + swap(mine[own:], "xh").astype(f32)


def body(tokens, doc_lengths, norm_gains, head_gains, q_o, kv_weight, ffn_weight, out_grad):
    rows = tokens.shape[0]
    dim = tokens.shape[1]
    head_dim = head_gains.shape[0]
    score_scale = head_dim ** (-0.5)
    xl = lax.axis_index("xl")
    c = lax.axis_index("c")
    dp_rows = q_o.shape[0]
    ff = ffn_weight.shape[2]
    ff_pad = -ff % 256
    wide = ff + ff_pad

    kv_half = lax.dynamic_slice_in_dim(kv_weight, c * head_dim, head_dim, 1)
    small = jnp.concatenate([q_o[:, 0, :], kv_half, q_o[:, 1, :]], axis=1)
    ffn_own = jnp.pad(ffn_weight, ((0, 0), (0, 0), (0, ff_pad))).reshape(dp_rows, 3 * wide)
    from_xl, ffn_other = lax.optimization_barrier((swap(small, "xl"), swap(ffn_own, "xl")))
    ffn_pair = jnp.concatenate([ffn_own, ffn_other], axis=0)
    pair = jnp.concatenate([small, from_xl], axis=0)
    qkv_half = gathered(pair[:, : 2 * head_dim])
    qkv_half, out_pair = lax.optimization_barrier((qkv_half, pair[:, 2 * head_dim :]))
    w_qkv_a = jnp.concatenate(
        [qkv_half[:, :head_dim], swap(qkv_half[:, :head_dim], "xh"), qkv_half[:, head_dim:]],
        axis=1,
    )
    w_qkv_b = swap(w_qkv_a, "c")
    out_half = gathered(out_pair)
    out_a = jnp.concatenate([out_half, swap(out_half, "xh")], axis=1)
    out_b = swap(out_a, "c")
    ffn_full = lax.all_gather(ffn_pair, ZY, axis=0, tiled=True)

    new = jnp.arange(dim, dtype=jnp.int32)
    z_of, y_of = new // (dp_rows * NXL * NY), (new // (dp_rows * NXL)) % NY
    xl_of = jnp.bitwise_xor((new // dp_rows) % NXL, xl)
    old = ((z_of * NXL + xl_of) * NY + y_of) * dp_rows + new % dp_rows
    order = (jnp.arange(dim, dtype=jnp.int32)[:, None] == old[None, :]).astype(bf16)

    def reordered(array):
        tail = array.shape[1:]
        cut = array.reshape(NZ, NXL, NY, dp_rows, *tail)
        first = jnp.where(xl == 0, cut[:, 0], cut[:, 1])
        second = jnp.where(xl == 0, cut[:, 1], cut[:, 0])
        return jnp.stack([first, second], axis=2).reshape(dim, *tail)

    gains = reordered(norm_gains)
    inputs = matmul(tokens, order)
    upstream = matmul(out_grad, order)

    block = ((lax.axis_index("z") * NXL + xl) * NY + lax.axis_index("y")) * NXH * NC
    block = block + lax.axis_index("xh") * NC + c
    back = WINDOW // rows
    key_index = (block - back) * rows + jnp.arange((back + 1) * rows, dtype=jnp.int32)
    key_doc, key_position = document_of(doc_lengths, key_index)
    key_doc = jnp.where(key_index < 0, -1, key_doc)
    query_index = key_index[back * rows :]
    query_doc = key_doc[back * rows :]
    cosine, sine_table = rope_tables(key_position[back * rows :], head_dim)
    distance = query_index[:, None] - key_index[None, :]
    allowed = (query_doc[:, None] == key_doc[None, :]) & (distance >= 0) & (distance < WINDOW)

    normed = rms_scale(inputs, gains[:, 0]).astype(bf16)
    qkv_a = matmul(normed, w_qkv_a)
    qkv_b = matmul(normed, w_qkv_b)
    query_raw = jnp.stack(
        [
            qkv_a[:, :head_dim],
            qkv_a[:, head_dim : 2 * head_dim],
            qkv_b[:, :head_dim],
            qkv_b[:, head_dim : 2 * head_dim],
        ],
        axis=0,
    )
    kv_a, kv_b = qkv_a[:, 2 * head_dim :], qkv_b[:, 2 * head_dim :]
    key_raw = jnp.where(c == 0, kv_a, kv_b)
    value_low = jnp.where(c == 0, kv_b, kv_a).astype(bf16)
    key_rot = rotate(rms_scale(key_raw, head_gains[:, 1]), cosine, sine_table).astype(bf16)
    packed = jnp.concatenate([key_rot, value_low], axis=1)
    both = jnp.concatenate([shifted(packed, by) for by in range(back, 0, -1)] + [packed], axis=0)
    key_all, value_all = both[:, :head_dim], both[:, head_dim:]
    query_rot = rotate(rms_scale(query_raw, head_gains[:, 0]), cosine, sine_table).astype(bf16)
    heads = query_raw.shape[0]
    query_flat = query_rot.reshape(heads * rows, head_dim)
    scores = matmul_nt(query_flat, key_all).reshape(heads, rows, -1) * score_scale
    scores = jnp.where(allowed[None], scores, masked_score)
    top_score = jnp.max(scores, axis=2, keepdims=True)
    weights = jnp.exp(scores - top_score)
    total = jnp.sum(weights, axis=2, keepdims=True)
    probs_full = (weights / total).reshape(heads * rows, -1)
    probs = probs_full.astype(bf16)
    attended = matmul(probs, value_all).astype(bf16).reshape(heads, rows, head_dim)
    attended_a = jnp.concatenate([attended[0], attended[1]], axis=1)
    attended_b = jnp.concatenate([attended[2], attended[3]], axis=1)
    attn_out = matmul_nt(attended_a, out_a) + matmul_nt(attended_b, out_b)
    resid = inputs + rms_scale(attn_out, gains[:, 1])

    ffn_in = group_rows(rms_scale(resid, gains[:, 2]).astype(bf16))
    w_gate, w_up, w_down = ffn_full[:, :wide], ffn_full[:, wide : 2 * wide], ffn_full[:, 2 * wide :]
    gate_up = matmul(ffn_in, ffn_full[:, : 2 * wide])
    gate_val, up_val = gate_up[:, :wide], gate_up[:, wide:]
    hidden = geglu(gate_val, up_val).astype(bf16)
    ffn_out = group_sum(matmul_nt(hidden, w_down).astype(bf16))
    mixed = (resid + rms_scale(ffn_out, gains[:, 3])).astype(bf16)
    grad_ffn_out, gain_three = norm_back(ffn_out, gains[:, 3], upstream)
    grad_ffn = group_rows(grad_ffn_out.astype(bf16))
    grad_hidden = matmul(grad_ffn, w_down)
    unused_value, pull = jax.vjp(geglu, gate_val, up_val)
    grad_gate, grad_up = pull(grad_hidden)
    grad_gate_up = jnp.concatenate([grad_gate.astype(bf16), grad_up.astype(bf16)], axis=1)
    grad_ffn_in = group_sum(matmul_nt(grad_gate_up, ffn_full[:, : 2 * wide]).astype(bf16))
    grad_w = jnp.concatenate(
        [matmul_tn(ffn_in, grad_gate_up).astype(bf16), matmul_tn(grad_ffn, hidden).astype(bf16)],
        axis=1,
    )
    ffn_rows = lax.psum_scatter(
        grad_w.reshape(NZ * NY, NXL * dp_rows, 3 * wide), ZY, scatter_dimension=0, tiled=False
    )
    ffn_rows = lax.optimization_barrier(ffn_rows)

    grad_from_ffn, gain_two = norm_back(resid, gains[:, 2], grad_ffn_in)
    grad_resid = upstream + grad_from_ffn
    grad_attn_out, gain_one = norm_back(attn_out, gains[:, 1], grad_resid)
    grad_attn = grad_attn_out.astype(bf16)

    def over_x(own, other):
        other = swap(other.astype(bf16), "c").astype(f32)
        chip = own.astype(f32) + other
        near, far = chip[:, :head_dim], chip[:, head_dim:]
        zy = summed([near, swap(far.astype(bf16), "xh")])
        return zy[:dp_rows] + swap(zy[dp_rows:].astype(bf16), "xl").astype(f32)

    out_share = over_x(matmul_tn(grad_attn, attended_a), matmul_tn(grad_attn, attended_b))

    att_grad_a = matmul(grad_attn, out_a).astype(bf16)
    att_grad_b = matmul(grad_attn, out_b).astype(bf16)
    grad_attended = jnp.concatenate(
        [
            att_grad_a[:, :head_dim],
            att_grad_a[:, head_dim:],
            att_grad_b[:, :head_dim],
            att_grad_b[:, head_dim:],
        ],
        axis=0,
    )
    grad_value_all = matmul_tn(probs, grad_attended)
    grad_probs = matmul_nt(grad_attended, value_all)
    inner = jnp.sum(probs_full * grad_probs, axis=1, keepdims=True)
    grad_scores = (probs_full * (grad_probs - inner)).astype(bf16)
    grad_query_rot = (matmul(grad_scores, key_all) * score_scale).reshape(heads, rows, head_dim)
    grad_key_all = matmul_tn(grad_scores, query_flat) * score_scale
    grad_query_norm = rotate(grad_query_rot, cosine, -sine_table)
    grad_query_raw, gain_query = norm_back(query_raw, head_gains[:, 0], grad_query_norm)
    grad_query = grad_query_raw.astype(bf16)
    key_grads = jnp.concatenate([grad_key_all, grad_value_all], axis=1)
    grad_qa = jnp.concatenate([grad_query[0], grad_query[1]], axis=1)
    grad_qb = jnp.concatenate([grad_query[2], grad_query[3]], axis=1)
    query_share = over_x(matmul_tn(normed, grad_qa), matmul_tn(normed, grad_qb))
    own_grads = key_grads[back * rows :]
    key_low = key_grads[: back * rows].astype(bf16)
    for by in range(1, back + 1):
        part = key_low[(back - by) * rows : (back - by + 1) * rows]
        own_grads = own_grads + shifted(part, -by).astype(f32)
    grad_key_norm = rotate(own_grads[:, :head_dim], cosine, -sine_table)
    grad_key_raw, gain_key = norm_back(key_raw, head_gains[:, 1], grad_key_norm)
    grad_key = grad_key_raw.astype(bf16)
    grad_value = own_grads[:, head_dim:].astype(bf16)
    grad_kv_a = jnp.where(c == 0, grad_key, grad_value)
    grad_kv_b = jnp.where(c == 0, grad_value, grad_key)
    grad_qkv_a = jnp.concatenate([grad_qa, grad_kv_a], axis=1)
    grad_qkv_b = jnp.concatenate([grad_qb, grad_kv_b], axis=1)
    grad_normed = matmul_nt(grad_qkv_a, w_qkv_a) + matmul_nt(grad_qkv_b, w_qkv_b)
    grad_from_norm, gain_zero = norm_back(inputs, gains[:, 0], grad_normed)
    tokens_grad = (grad_resid + grad_from_norm).astype(bf16)

    norm_part = jnp.stack(
        [jnp.sum(g, axis=0) for g in (gain_zero, gain_one, gain_two, gain_three)], axis=1
    )
    head_part = jnp.stack([jnp.sum(gain_query, axis=(0, 1)), jnp.sum(gain_key, axis=0)], axis=1)
    head_cut = head_part.reshape(NZ, NXL, NY, -1)
    head_cut = jnp.stack(
        [
            jnp.where(xl == 0, head_cut[:, 0], head_cut[:, 1]),
            jnp.where(xl == 0, head_cut[:, 1], head_cut[:, 0]),
        ],
        axis=2,
    )
    per_dp = head_cut.shape[-1]
    head_column = jnp.pad(head_cut, ((0, 0), (0, 0), (0, 0), (0, dp_rows - per_dp)))
    gain_cols = jnp.concatenate([norm_part, head_column.reshape(dim, 1)], axis=1)
    n_gain = gain_cols.shape[1]
    gain_cols = jnp.pad(gain_cols, ((0, 0), (0, 128 - n_gain))).astype(bf16)

    kv_gain_a = jnp.concatenate([matmul_tn(normed, grad_kv_a).astype(bf16), gain_cols], axis=1)
    kv_gain_b = jnp.concatenate([matmul_tn(normed, grad_kv_b).astype(bf16), gain_cols], axis=1)
    kv_zy = summed([kv_gain_a, swap(kv_gain_b, "c")]).astype(bf16)
    near, far = kv_zy[:dp_rows], kv_zy[dp_rows:]
    x_sum = (
        near.astype(f32)
        + swap(far, "xl").astype(f32)
        + swap(near, "xh").astype(f32)
        + swap_both(far).astype(f32)
    )
    qo_share = jnp.stack([query_share, out_share], axis=1)
    kv_mine = x_sum[:, :head_dim]
    kv_other = swap(kv_mine.astype(bf16), "c").astype(f32)
    kv_mine = kv_mine.astype(bf16).astype(f32)
    kv_total = jnp.concatenate(
        [jnp.where(c == 0, kv_mine, kv_other), jnp.where(c == 0, kv_other, kv_mine)], axis=1
    )
    norm_total = x_sum[:, head_dim : head_dim + 4]
    head_total = x_sum[:per_dp, head_dim + 4].reshape(-1, 2)

    ffn_share = ffn_rows[:dp_rows].astype(f32) + swap(ffn_rows[dp_rows:], "xl").astype(f32)
    ffn_share = ffn_share.reshape(dp_rows, 3, wide)[:, :, :ff]

    def restored(array):
        return matmul_nt(array, order).astype(bf16)

    return (
        restored(mixed),
        restored(tokens_grad),
        norm_total,
        head_total,
        qo_share,
        kv_total,
        ffn_share,
    )


def solution(mesh):
    fine = Mesh(np.asarray(mesh.devices).reshape(NZ, NXL, NY, NXH, NC), ALL)
    dp, tensor = ("z", "xl", "y"), ("xh", "c")
    return jax.shard_map(
        body,
        mesh=fine,
        in_specs=(
            P(ALL, None),
            P(),
            P(),
            P(),
            P(dp, None, tensor),
            P(dp, None),
            P(dp, None, tensor),
            P(ALL, None),
        ),
        out_specs=(
            P(ALL, None),
            P(ALL, None),
            P(dp, None),
            P(dp, None),
            P(dp, None, tensor),
            P(dp, None),
            P(dp, None, tensor),
        ),
        check_vma=False,
    )
```

```python
import jax
import jax.numpy as jnp
import numpy as np
from jax import lax
from jax.experimental import pallas as pl
from jax.experimental.pallas import tpu as pltpu
from jax.sharding import Mesh
from jax.sharding import PartitionSpec as P

WINDOW = 512
NZ, NXL, NY, NXH, NC = 4, 2, 4, 2, 2
ALL = ("z", "xl", "y", "xh", "c")
ZY = ("z", "y")
BLOCKS = NZ * NXL * NY * NXH * NC

epsilon = 1e-06
rope_base = 10000.0
masked_score = -1e30
bf16 = jnp.bfloat16
f32 = jnp.float32


def rms_scale(values, gains):
    mean_square = jnp.mean(values * values, axis=-1, keepdims=True)
    return values * lax.rsqrt(mean_square + epsilon) * (1.0 + gains)


def norm_back(values, gains, upstream):
    inverse = lax.rsqrt(jnp.mean(values * values, axis=-1, keepdims=True) + epsilon)
    normed = values * inverse
    scaled = upstream * (1.0 + gains)
    grad_values = inverse * (scaled - normed * jnp.mean(scaled * normed, axis=-1, keepdims=True))
    return (grad_values, upstream * normed)


def rotate(values, cosine, sine_table):
    half_dim = values.shape[-1] // 2
    front = values[..., :half_dim]
    back_half = values[..., half_dim:]
    return jnp.concatenate(
        [front * cosine - back_half * sine_table, back_half * cosine + front * sine_table], axis=-1
    )


def rope_tables(position, head_dim):
    half_dim = head_dim // 2
    exponent = jnp.arange(half_dim).astype(f32) * (-2.0 / head_dim)
    frequency = jnp.power(f32(rope_base), exponent)
    angle = position.astype(f32)[:, None] * frequency[None, :]
    return (jnp.cos(angle), jnp.sin(angle))


def document_of(doc_lengths, index):
    ends = jnp.cumsum(doc_lengths)
    starts = ends - doc_lengths
    doc_number = jnp.sum((ends[None, :] <= index[:, None]).astype(jnp.int32), axis=1)
    owner = doc_number[:, None] == jnp.arange(doc_lengths.shape[0], dtype=jnp.int32)[None, :]
    position = index - jnp.sum(jnp.where(owner, starts[None, :], 0), axis=1)
    return (doc_number, position)


def geglu(gate_in, up_in):
    return jax.nn.gelu(gate_in, approximate=True) * up_in


def matmul(left, right):
    return jnp.dot(left, right, preferred_element_type=f32)


def matmul_nt(left, right):
    return lax.dot_general(left, right, (((1,), (1,)), ((), ())), preferred_element_type=f32)


def matmul_tn(left, right):
    return lax.dot_general(left, right, (((0,), (0,)), ((), ())), preferred_element_type=f32)


def swap(array, axis):
    return lax.ppermute(array, axis, [(0, 1), (1, 0)])


def swap_both(array):
    return lax.ppermute(array, ("xl", "xh"), [(0, 3), (1, 2), (2, 1), (3, 0)])


def shifted(array, by):
    return lax.ppermute(
        array, ALL, [(i, i + by) for i in range(BLOCKS) if 0 <= i + by < BLOCKS]
    )


def gathered(own):
    blocks = jnp.broadcast_to(own[None], (NZ * NY, *own.shape))
    return lax.all_to_all(blocks, ZY, 0, 0, tiled=True).reshape(-1, own.shape[1])


def summed(whole):
    blocks = whole.reshape(NZ * NY, -1, whole.shape[1])
    arrived = lax.all_to_all(blocks, ZY, 0, 0, tiled=True)
    return jnp.sum(arrived.astype(f32), axis=0)


def from_x(near, far):
    own = near.shape[0] // 2
    return (
        near[:own].astype(f32)
        + swap(near[own:], "xl").astype(f32)
        + swap(far[:own], "xh").astype(f32)
        + swap_both(far[own:]).astype(f32)
    ).astype(bf16)


def exact(left, right):
    return lax.dot_general(
        left, right.astype(f32), (((1,), (1,)), ((), ())), precision=lax.Precision.HIGHEST
    )


def weight_sums(ffn_in, grads, grad_out, hidden):
    rows, dim = ffn_in[0].shape
    width = hidden[0].shape[1] // 2
    first = grads[0].shape[1] // width

    def kernel(in_near, in_far, out_near, out_far, g_near, g_far, h_near, h_far, sums):
        def both(left, right):
            sums[...] = sum(matmul_tn(a[...], b[...]) for a, b in zip(left, right)).astype(bf16)

        @pl.when(pl.program_id(0) < first)
        def _():
            both((in_near, in_far), (g_near, g_far))

        @pl.when(pl.program_id(0) >= first)
        def _():
            both((out_near, out_far), (h_near, h_far))

    whole = pl.BlockSpec((rows, dim), lambda i: (0, 0))
    grad_tile = pl.BlockSpec((rows, width), lambda i: (0, jnp.minimum(i, first - 1)))
    hidden_tile = pl.BlockSpec((rows, width), lambda i: (0, jnp.maximum(i - first, 0)))
    return pl.pallas_call(
        kernel,
        grid=(first + 2,),
        out_shape=jax.ShapeDtypeStruct((dim, (first + 2) * width), bf16),
        in_specs=[whole] * 4 + [grad_tile] * 2 + [hidden_tile] * 2,
        out_specs=pl.BlockSpec((dim, width), lambda i: (0, i)),
        compiler_params=pltpu.CompilerParams(vmem_limit_bytes=40 * 2**20),
        cost_estimate=pl.CostEstimate(
            flops=4 * rows * dim * (first + 2) * width,
            bytes_accessed=2 * (first + 2) * width * (dim + 2 * rows),
            transcendentals=0,
        ),
    )(*ffn_in, *grad_out, *grads, *hidden)


def over_cores(part):
    own = part.shape[0] // 2
    return part[:own].astype(f32) + swap(part[own:], "c").astype(f32)


def group_rows(own):
    far = swap(own, "xh")
    return (
        jnp.concatenate([own, swap(own, "c")], axis=0),
        jnp.concatenate([far, swap(far, "c")], axis=0),
    )


def body(tokens, doc_lengths, norm_gains, head_gains, q_o, kv_weight, ffn_weight, out_grad):
    rows = tokens.shape[0]
    dim = tokens.shape[1]
    head_dim = head_gains.shape[0]
    score_scale = head_dim ** (-0.5)
    xl = lax.axis_index("xl")
    c = lax.axis_index("c")
    dp_rows = q_o.shape[0]
    ff = ffn_weight.shape[2]
    ff_pad = -ff % 256
    wide = ff + ff_pad

    kv_half = lax.dynamic_slice_in_dim(kv_weight, c * head_dim, head_dim, 1)
    small = jnp.concatenate([q_o[:, 0, :], kv_half, q_o[:, 1, :]], axis=1)
    ffn_own = jnp.pad(ffn_weight, ((0, 0), (0, 0), (0, ff_pad))).reshape(dp_rows, 3 * wide)
    ffn_other = swap(ffn_own, "xl")
    ffn_pair = jnp.concatenate([ffn_own, ffn_other], axis=0)
    quarter = gathered(small)
    q_own, kv_own, o_own = (quarter[:, k * head_dim : (k + 1) * head_dim] for k in range(3))

    def rows_of(own, other):
        return jnp.concatenate([own, other], axis=0)

    kv_a = rows_of(kv_own, swap(kv_own, "xl"))
    kv_b = swap(kv_a, "c")
    q_near = rows_of(q_own, swap(q_own, "xl"))
    q_far = rows_of(swap(q_own, "xh"), swap_both(q_own))
    ffn_full = lax.all_gather(ffn_pair, ZY, axis=0, tiled=True)

    place = jnp.arange(dim, dtype=jnp.int32)
    row = place % dp_rows

    def one_hot(source):
        return (place[:, None] == source[None, :]).astype(bf16)

    def source(z_of, y_of, side):
        return ((z_of * NXL + jnp.bitwise_xor(side, xl)) * NY + y_of) * dp_rows + row

    step = place // dp_rows
    order = one_hot(source(step // (NXL * NY), (step // NXL) % NY, step % NXL))
    order_a = one_hot(source((step // NY) % NZ, step % NY, step // (NZ * NY)))
    to_attn = one_hot(((step % (NZ * NY)) * NXL + step // (NZ * NY)) * dp_rows + row)

    def sides(array):
        cut = array.reshape(NZ, NXL, NY, *array.shape[1:])
        first = jnp.where(xl == 0, cut[:, 0], cut[:, 1])
        second = jnp.where(xl == 0, cut[:, 1], cut[:, 0])
        return first, second

    gain_sides = sides(norm_gains.reshape(NZ * NXL * NY, dp_rows, -1))
    gains = jnp.stack(gain_sides, axis=2).reshape(norm_gains.shape)
    gains_a = jnp.stack(gain_sides, axis=0).reshape(norm_gains.shape)
    inputs = matmul(tokens, order)
    inputs_a = matmul(tokens, order_a)
    upstream = matmul(out_grad, order)

    block = ((lax.axis_index("z") * NXL + xl) * NY + lax.axis_index("y")) * NXH * NC
    block = block + lax.axis_index("xh") * NC + c
    back = WINDOW // rows
    key_index = (block - back) * rows + jnp.arange((back + 1) * rows, dtype=jnp.int32)
    key_doc, key_position = document_of(doc_lengths, key_index)
    key_doc = jnp.where(key_index < 0, -1, key_doc)
    query_index = key_index[back * rows :]
    query_doc = key_doc[back * rows :]
    cosine, sine_table = rope_tables(key_position[back * rows :], head_dim)
    distance = query_index[:, None] - key_index[None, :]
    allowed = (query_doc[:, None] == key_doc[None, :]) & (distance >= 0) & (distance < WINDOW)

    normed = rms_scale(inputs_a, gains_a[:, 0]).astype(bf16)
    from_a, from_b = matmul(normed, kv_a), matmul(normed, kv_b)
    key_raw = jnp.where(c == 0, from_a, from_b)
    value_low = jnp.where(c == 0, from_b, from_a).astype(bf16)
    key_rot = rotate(rms_scale(key_raw, head_gains[:, 1]), cosine, sine_table).astype(bf16)
    packed = jnp.concatenate([key_rot, value_low], axis=1)
    both = jnp.concatenate([shifted(packed, by) for by in range(back, 0, -1)] + [packed], axis=0)
    key_all, value_all = both[:, :head_dim], both[:, head_dim:]
    q_near, q_far, o_own = lax.optimization_barrier((q_near, q_far, o_own))
    o_near = rows_of(o_own, swap(o_own, "xl"))
    o_far = rows_of(swap(o_own, "xh"), swap_both(o_own))
    w_query = (q_near, q_far, swap(q_near, "c"), swap(q_far, "c"))
    query_raw = jnp.stack([matmul(normed, w) for w in w_query], axis=0)
    query_rot = rotate(rms_scale(query_raw, head_gains[:, 0]), cosine, sine_table).astype(bf16)
    heads = query_raw.shape[0]
    query_flat = query_rot.reshape(heads * rows, head_dim)
    scores = matmul_nt(query_flat, key_all).reshape(heads, rows, -1) * score_scale
    scores = jnp.where(allowed[None], scores, masked_score)
    top_score = jnp.max(scores, axis=2, keepdims=True)
    weights = jnp.exp(scores - top_score)
    total = jnp.sum(weights, axis=2, keepdims=True)
    probs_full = (weights / total).reshape(heads * rows, -1)
    probs = probs_full.astype(bf16)
    attended = matmul(probs, value_all).astype(bf16).reshape(heads, rows, head_dim)
    attended, o_near, o_far = lax.optimization_barrier((attended, o_near, o_far))
    w_out = (o_near, o_far, swap(o_near, "c"), swap(o_far, "c"))
    attn_out = exact(sum(matmul_nt(a, w) for a, w in zip(attended, w_out)), to_attn)
    resid = inputs + rms_scale(attn_out, gains[:, 1])

    ffn_in = group_rows(rms_scale(resid, gains[:, 2]).astype(bf16))
    w_gate_up, w_down = ffn_full[:, : 2 * wide], ffn_full[:, 2 * wide :]

    def forward(rows_in):
        gate_up = matmul(rows_in, w_gate_up)
        gate_val, up_val = gate_up[:, :wide], gate_up[:, wide:]
        hidden = geglu(gate_val, up_val).astype(bf16)
        return gate_val, up_val, hidden, matmul_nt(hidden, w_down).astype(bf16)

    far_kept = forward(ffn_in[1])
    far_sum = over_cores(far_kept[3]).astype(bf16)
    near_in, far_sum = lax.optimization_barrier((ffn_in[0], far_sum))
    kept = (forward(near_in), far_kept)
    ffn_out = over_cores(kept[0][3]) + swap(far_sum, "xh").astype(f32)
    mixed = (resid + rms_scale(ffn_out, gains[:, 3])).astype(bf16)
    grad_ffn_out, gain_three = norm_back(ffn_out, gains[:, 3], upstream)
    grad_own = grad_ffn_out.astype(bf16)
    grad_far = swap(grad_own, "xh")
    grad_near = jnp.concatenate([grad_own, swap(grad_own, "c")], axis=0)

    def backward(rows_in, gate_val, up_val):
        unused_value, pull = jax.vjp(geglu, gate_val, up_val)
        grad_gate, grad_up = pull(matmul(rows_in, w_down))
        return jnp.concatenate([grad_gate.astype(bf16), grad_up.astype(bf16)], axis=1)

    near_pulled = backward(grad_near, kept[0][0], kept[0][1])
    near_pulled, grad_far = lax.optimization_barrier((near_pulled, grad_far))
    grad_ffn = (grad_near, jnp.concatenate([grad_far, swap(grad_far, "c")], axis=0))
    far_pulled = backward(grad_ffn[1], kept[1][0], kept[1][1])
    far_sum = over_cores(matmul_nt(far_pulled, w_gate_up).astype(bf16)).astype(bf16)
    near_pulled, far_pulled, far_sum = lax.optimization_barrier(
        (near_pulled, far_pulled, far_sum)
    )
    grad_w = weight_sums(
        ffn_in, (near_pulled, far_pulled), grad_ffn, tuple(k[2] for k in kept)
    )
    near_part = matmul_nt(near_pulled, w_gate_up).astype(bf16)
    grad_ffn_in = over_cores(near_part) + swap(far_sum, "xh").astype(f32)

    ffn_rows = lax.psum_scatter(
        grad_w.reshape(NZ * NY, NXL * dp_rows, 3 * wide), ZY, scatter_dimension=0, tiled=False
    )
    ffn_rows = lax.optimization_barrier(ffn_rows)

    grad_from_ffn, gain_two = norm_back(resid, gains[:, 2], grad_ffn_in)
    grad_resid = upstream + grad_from_ffn
    grad_attn_out, gain_one = norm_back(attn_out, gains[:, 1], grad_resid)
    grad_attn = grad_attn_out.astype(bf16)

    grad_attn = matmul(grad_attn, to_attn).astype(bf16)

    def chip_sums(left, rights):
        sums = [matmul_tn(left, r).astype(bf16) for r in rights]
        half = len(sums) // 2
        return [
            (mine.astype(f32) + swap(sent, "c").astype(f32)).astype(bf16)
            for mine, sent in zip(sums[:half], sums[half:])
        ]

    out_near, out_far = chip_sums(grad_attn, attended)

    grad_attended = jnp.concatenate([matmul(grad_attn, w).astype(bf16) for w in w_out], axis=0)
    grad_value_all = matmul_tn(probs, grad_attended)
    grad_probs = matmul_nt(grad_attended, value_all)
    inner = jnp.sum(probs_full * grad_probs, axis=1, keepdims=True)
    grad_scores = (probs_full * (grad_probs - inner)).astype(bf16)
    grad_scores, out_near, out_far = lax.optimization_barrier((grad_scores, out_near, out_far))
    out_sum = from_x(out_near, out_far)
    grad_query_rot = (matmul(grad_scores, key_all) * score_scale).reshape(heads, rows, head_dim)
    grad_key_all = matmul_tn(grad_scores, query_flat) * score_scale
    grad_query_norm = rotate(grad_query_rot, cosine, -sine_table)
    grad_query_raw, gain_query = norm_back(query_raw, head_gains[:, 0], grad_query_norm)
    grad_query = grad_query_raw.astype(bf16)
    key_grads = jnp.concatenate([grad_key_all, grad_value_all], axis=1)
    query_sum = from_x(*chip_sums(normed, grad_query))
    own_grads = key_grads[back * rows :]
    key_low = key_grads[: back * rows].astype(bf16)
    for by in range(1, back + 1):
        part = key_low[(back - by) * rows : (back - by + 1) * rows]
        own_grads = own_grads + shifted(part, -by).astype(f32)
    grad_key_norm = rotate(own_grads[:, :head_dim], cosine, -sine_table)
    grad_key_raw, gain_key = norm_back(key_raw, head_gains[:, 1], grad_key_norm)
    grad_key = grad_key_raw.astype(bf16)
    grad_value = own_grads[:, head_dim:].astype(bf16)
    grad_kv_a = jnp.where(c == 0, grad_key, grad_value)
    grad_kv_b = jnp.where(c == 0, grad_value, grad_key)
    grad_normed = sum(matmul_nt(g, w) for g, w in zip(grad_query, w_query))
    grad_normed = grad_normed + matmul_nt(grad_kv_a, kv_a) + matmul_nt(grad_kv_b, kv_b)
    grad_from_norm, gain_zero = norm_back(inputs_a, gains_a[:, 0], grad_normed)
    tokens_grad = (exact(grad_resid, order) + exact(grad_from_norm, order_a)).astype(bf16)

    late_gains = jnp.stack([jnp.sum(g, axis=0) for g in (gain_one, gain_two, gain_three)], axis=0)
    late_gains = lax.dot(late_gains, to_attn.astype(f32), precision=lax.Precision.HIGHEST)
    norm_part = jnp.concatenate([jnp.sum(gain_zero, axis=0)[None], late_gains], axis=0).T
    head_part = jnp.stack([jnp.sum(gain_query, axis=(0, 1)), jnp.sum(gain_key, axis=0)], axis=1)
    head_cut = jnp.stack(sides(head_part.reshape(NZ * NXL * NY, -1)), axis=0)
    per_dp = head_cut.shape[-1]
    head_column = jnp.pad(head_cut, ((0, 0), (0, 0), (0, 0), (0, dp_rows - per_dp)))
    gain_cols = jnp.concatenate([norm_part, head_column.reshape(dim, 1)], axis=1)
    n_gain = gain_cols.shape[1]
    gain_cols = jnp.pad(gain_cols, ((0, 0), (0, 128 - n_gain))).astype(bf16)

    kv_gain_a = jnp.concatenate([matmul_tn(normed, grad_kv_a).astype(bf16), gain_cols], axis=1)
    kv_gain_b = jnp.concatenate([matmul_tn(normed, grad_kv_b).astype(bf16), gain_cols], axis=1)
    kv_gain = kv_gain_a.astype(f32) + swap(kv_gain_b, "c").astype(f32)
    own = dim // 2
    kv_gain = kv_gain[:own] + swap(kv_gain[own:].astype(bf16), "xl").astype(f32)
    late = summed(jnp.concatenate([query_sum, out_sum, kv_gain.astype(bf16)], axis=1))
    late, ffn_rows = lax.optimization_barrier((late, ffn_rows))
    qo_share = late[:, : 2 * head_dim].reshape(dp_rows, 2, head_dim)
    x_sum = late[:, 2 * head_dim :].astype(bf16)
    x_sum = x_sum.astype(f32) + swap(x_sum, "xh").astype(f32)
    kv_mine = x_sum[:, :head_dim]
    kv_other = swap(kv_mine.astype(bf16), "c").astype(f32)
    kv_mine = kv_mine.astype(bf16).astype(f32)
    kv_total = jnp.concatenate(
        [jnp.where(c == 0, kv_mine, kv_other), jnp.where(c == 0, kv_other, kv_mine)], axis=1
    )
    norm_total = x_sum[:, head_dim : head_dim + 4]
    head_total = x_sum[:per_dp, head_dim + 4].reshape(-1, 2)

    ffn_share = ffn_rows[:dp_rows].astype(f32) + swap(ffn_rows[dp_rows:], "xl").astype(f32)
    ffn_share = ffn_share.reshape(dp_rows, 3, wide)[:, :, :ff]

    return (
        matmul_nt(mixed, order).astype(bf16),
        tokens_grad,
        norm_total,
        head_total,
        qo_share,
        kv_total,
        ffn_share,
    )


def solution(mesh):
    fine = Mesh(np.asarray(mesh.devices).reshape(NZ, NXL, NY, NXH, NC), ALL)
    dp, tensor = ("z", "xl", "y"), ("xh", "c")
    return jax.shard_map(
        body,
        mesh=fine,
        in_specs=(
            P(ALL, None),
            P(),
            P(),
            P(),
            P(dp, None, tensor),
            P(dp, None),
            P(dp, None, tensor),
            P(ALL, None),
        ),
        out_specs=(
            P(ALL, None),
            P(ALL, None),
            P(dp, None),
            P(dp, None),
            P(dp, None, tensor),
            P(dp, None),
            P(dp, None, tensor),
        ),
        check_vma=False,
    )
```

```python
import jax
import jax.numpy as jnp
import numpy as np
from jax import lax
from jax.experimental import pallas as pl
from jax.experimental.pallas import tpu as pltpu
from jax.sharding import Mesh
from jax.sharding import PartitionSpec as P

WINDOW = 512
NZ, NXL, NY, NXH, NC = 4, 2, 4, 2, 2
ALL = ("z", "xl", "y", "xh", "c")
ZY = ("z", "y")
BLOCKS = NZ * NXL * NY * NXH * NC

epsilon = 1e-06
rope_base = 10000.0
masked_score = -1e30
bf16 = jnp.bfloat16
f32 = jnp.float32


def rms_scale(values, gains):
    mean_square = jnp.mean(values * values, axis=-1, keepdims=True)
    return values * lax.rsqrt(mean_square + epsilon) * (1.0 + gains)


def norm_back(values, gains, upstream):
    inverse = lax.rsqrt(jnp.mean(values * values, axis=-1, keepdims=True) + epsilon)
    normed = values * inverse
    scaled = upstream * (1.0 + gains)
    grad_values = inverse * (scaled - normed * jnp.mean(scaled * normed, axis=-1, keepdims=True))
    return (grad_values, upstream * normed)


def rotate(values, cosine, sine_table):
    half_dim = values.shape[-1] // 2
    front = values[..., :half_dim]
    back_half = values[..., half_dim:]
    return jnp.concatenate(
        [front * cosine - back_half * sine_table, back_half * cosine + front * sine_table], axis=-1
    )


def rope_tables(position, head_dim):
    half_dim = head_dim // 2
    exponent = jnp.arange(half_dim).astype(f32) * (-2.0 / head_dim)
    frequency = jnp.power(f32(rope_base), exponent)
    angle = position.astype(f32)[:, None] * frequency[None, :]
    return (jnp.cos(angle), jnp.sin(angle))


def document_of(doc_lengths, index):
    ends = jnp.cumsum(doc_lengths)
    starts = ends - doc_lengths
    doc_number = jnp.sum((ends[None, :] <= index[:, None]).astype(jnp.int32), axis=1)
    owner = doc_number[:, None] == jnp.arange(doc_lengths.shape[0], dtype=jnp.int32)[None, :]
    position = index - jnp.sum(jnp.where(owner, starts[None, :], 0), axis=1)
    return (doc_number, position)


def geglu(gate_in, up_in):
    return jax.nn.gelu(gate_in, approximate=True) * up_in


def matmul(left, right):
    return jnp.dot(left, right, preferred_element_type=f32)


def matmul_nt(left, right):
    return lax.dot_general(left, right, (((1,), (1,)), ((), ())), preferred_element_type=f32)


def matmul_tn(left, right):
    return lax.dot_general(left, right, (((0,), (0,)), ((), ())), preferred_element_type=f32)


def swap(array, axis):
    return lax.ppermute(array, axis, [(0, 1), (1, 0)])


def swap_both(array):
    return lax.ppermute(array, ("xl", "xh"), [(0, 3), (1, 2), (2, 1), (3, 0)])


def shifted(array, by):
    return lax.ppermute(
        array, ALL, [(i, i + by) for i in range(BLOCKS) if 0 <= i + by < BLOCKS]
    )


def gathered(own):
    blocks = jnp.broadcast_to(own[None], (NZ * NY, *own.shape))
    return lax.all_to_all(blocks, ZY, 0, 0, tiled=True).reshape(-1, own.shape[1])


def summed(whole):
    blocks = whole.reshape(NZ * NY, -1, whole.shape[1])
    arrived = lax.all_to_all(blocks, ZY, 0, 0, tiled=True)
    return jnp.sum(arrived.astype(f32), axis=0)


def from_x(near, far):
    own = near.shape[0] // 2
    return (
        near[:own].astype(f32)
        + swap(near[own:], "xl").astype(f32)
        + swap(far[:own], "xh").astype(f32)
        + swap_both(far[own:]).astype(f32)
    ).astype(bf16)


def exact(left, right):
    return lax.dot_general(
        left, right.astype(f32), (((1,), (1,)), ((), ())), precision=lax.Precision.HIGH
    )


def weight_sums(ffn_in, grads, grad_out, hidden):
    rows, dim = ffn_in[0].shape
    width = hidden[0].shape[1] // 2
    first = grads[0].shape[1] // width

    def kernel(in_near, in_far, out_near, out_far, g_near, g_far, h_near, h_far, sums):
        def both(left, right):
            sums[...] = sum(matmul_tn(a[...], b[...]) for a, b in zip(left, right)).astype(bf16)

        @pl.when(pl.program_id(0) < first)
        def _():
            both((in_near, in_far), (g_near, g_far))

        @pl.when(pl.program_id(0) >= first)
        def _():
            both((out_near, out_far), (h_near, h_far))

    whole = pl.BlockSpec((rows, dim), lambda i: (0, 0))
    grad_tile = pl.BlockSpec((rows, width), lambda i: (0, jnp.minimum(i, first - 1)))
    hidden_tile = pl.BlockSpec((rows, width), lambda i: (0, jnp.maximum(i - first, 0)))
    return pl.pallas_call(
        kernel,
        grid=(first + 2,),
        out_shape=jax.ShapeDtypeStruct((dim, (first + 2) * width), bf16),
        in_specs=[whole] * 4 + [grad_tile] * 2 + [hidden_tile] * 2,
        out_specs=pl.BlockSpec((dim, width), lambda i: (0, i)),
        compiler_params=pltpu.CompilerParams(vmem_limit_bytes=40 * 2**20),
        cost_estimate=pl.CostEstimate(
            flops=4 * rows * dim * (first + 2) * width,
            bytes_accessed=2 * (first + 2) * width * (dim + 2 * rows),
            transcendentals=0,
        ),
    )(*ffn_in, *grad_out, *grads, *hidden)


def over_cores(part):
    own = part.shape[0] // 2
    return part[:own].astype(f32) + swap(part[own:], "c").astype(f32)


def group_rows(own):
    far = swap(own, "xh")
    return (
        jnp.concatenate([own, swap(own, "c")], axis=0),
        jnp.concatenate([far, swap(far, "c")], axis=0),
    )


def body(tokens, doc_lengths, norm_gains, head_gains, q_o, kv_weight, ffn_weight, out_grad):
    rows = tokens.shape[0]
    dim = tokens.shape[1]
    head_dim = head_gains.shape[0]
    score_scale = head_dim ** (-0.5)
    xl = lax.axis_index("xl")
    c = lax.axis_index("c")
    dp_rows = q_o.shape[0]
    ff = ffn_weight.shape[2]
    ff_pad = -ff % 256
    wide = ff + ff_pad

    kv_half = lax.dynamic_slice_in_dim(kv_weight, c * head_dim, head_dim, 1)
    small = jnp.concatenate([q_o[:, 0, :], kv_half, q_o[:, 1, :]], axis=1)
    ffn_own = jnp.pad(ffn_weight, ((0, 0), (0, 0), (0, ff_pad))).reshape(dp_rows, 3 * wide)
    ffn_other = swap(ffn_own, "xl")
    ffn_pair = jnp.concatenate([ffn_own, ffn_other], axis=0)
    quarter = gathered(small)
    q_own, kv_own, o_own = (quarter[:, k * head_dim : (k + 1) * head_dim] for k in range(3))

    def rows_of(own, other):
        return jnp.concatenate([own, other], axis=0)

    kv_a = rows_of(kv_own, swap(kv_own, "xl"))
    kv_b = swap(kv_a, "c")
    q_near = rows_of(q_own, swap(q_own, "xl"))
    q_far = rows_of(swap(q_own, "xh"), swap_both(q_own))
    ffn_full = lax.all_gather(ffn_pair, ZY, axis=0, tiled=True)

    place = jnp.arange(dim, dtype=jnp.int32)
    row = place % dp_rows

    def one_hot(source):
        return (place[:, None] == source[None, :]).astype(bf16)

    def source(z_of, y_of, side):
        return ((z_of * NXL + jnp.bitwise_xor(side, xl)) * NY + y_of) * dp_rows + row

    step = place // dp_rows
    order = one_hot(source(step // (NXL * NY), (step // NXL) % NY, step % NXL))
    order_a = one_hot(source((step // NY) % NZ, step % NY, step // (NZ * NY)))
    to_attn = one_hot(((step % (NZ * NY)) * NXL + step // (NZ * NY)) * dp_rows + row)

    def sides(array):
        cut = array.reshape(NZ, NXL, NY, *array.shape[1:])
        first = jnp.where(xl == 0, cut[:, 0], cut[:, 1])
        second = jnp.where(xl == 0, cut[:, 1], cut[:, 0])
        return first, second

    gain_sides = sides(norm_gains.reshape(NZ * NXL * NY, dp_rows, -1))
    gains = jnp.stack(gain_sides, axis=2).reshape(norm_gains.shape)
    gains_a = jnp.stack(gain_sides, axis=0).reshape(norm_gains.shape)
    inputs = matmul(tokens, order)
    inputs_a = matmul(tokens, order_a)
    upstream = matmul(out_grad, order)
    inputs, inputs_a, upstream = lax.optimization_barrier((inputs, inputs_a, upstream))

    block = ((lax.axis_index("z") * NXL + xl) * NY + lax.axis_index("y")) * NXH * NC
    block = block + lax.axis_index("xh") * NC + c
    back = WINDOW // rows
    key_index = (block - back) * rows + jnp.arange((back + 1) * rows, dtype=jnp.int32)
    key_doc, key_position = document_of(doc_lengths, key_index)
    key_doc = jnp.where(key_index < 0, -1, key_doc)
    query_index = key_index[back * rows :]
    query_doc = key_doc[back * rows :]
    cosine, sine_table = rope_tables(key_position[back * rows :], head_dim)
    distance = query_index[:, None] - key_index[None, :]
    allowed = (query_doc[:, None] == key_doc[None, :]) & (distance >= 0) & (distance < WINDOW)

    normed = rms_scale(inputs_a, gains_a[:, 0]).astype(bf16)
    from_a, from_b = matmul(normed, kv_a), matmul(normed, kv_b)
    key_raw = jnp.where(c == 0, from_a, from_b)
    value_low = jnp.where(c == 0, from_b, from_a).astype(bf16)
    key_rot = rotate(rms_scale(key_raw, head_gains[:, 1]), cosine, sine_table).astype(bf16)
    packed = jnp.concatenate([key_rot, value_low], axis=1)
    both = jnp.concatenate([shifted(packed, by) for by in range(back, 0, -1)] + [packed], axis=0)
    key_all, value_all = both[:, :head_dim], both[:, head_dim:]
    q_near, q_far, o_own = lax.optimization_barrier((q_near, q_far, o_own))
    o_near = rows_of(o_own, swap(o_own, "xl"))
    o_far = rows_of(swap(o_own, "xh"), swap_both(o_own))
    w_query = (q_near, q_far, swap(q_near, "c"), swap(q_far, "c"))
    query_raw = jnp.stack([matmul(normed, w) for w in w_query], axis=0)
    query_rot = rotate(rms_scale(query_raw, head_gains[:, 0]), cosine, sine_table).astype(bf16)
    heads = query_raw.shape[0]
    query_flat = query_rot.reshape(heads * rows, head_dim)
    scores = matmul_nt(query_flat, key_all).reshape(heads, rows, -1) * score_scale
    scores = jnp.where(allowed[None], scores, masked_score)
    top_score = jnp.max(scores, axis=2, keepdims=True)
    weights = jnp.exp(scores - top_score)
    total = jnp.sum(weights, axis=2, keepdims=True)
    probs_full = (weights / total).reshape(heads * rows, -1)
    probs = probs_full.astype(bf16)
    attended = matmul(probs, value_all).astype(bf16).reshape(heads, rows, head_dim)
    attended, o_near, o_far = lax.optimization_barrier((attended, o_near, o_far))
    w_out = (o_near, o_far, swap(o_near, "c"), swap(o_far, "c"))
    attn_out = exact(sum(matmul_nt(a, w) for a, w in zip(attended, w_out)), to_attn)
    resid = inputs + rms_scale(attn_out, gains[:, 1])

    ffn_in = group_rows(rms_scale(resid, gains[:, 2]).astype(bf16))
    w_gate_up, w_down = ffn_full[:, : 2 * wide], ffn_full[:, 2 * wide :]

    def forward(rows_in):
        gate_up = matmul(rows_in, w_gate_up)
        gate_val, up_val = gate_up[:, :wide], gate_up[:, wide:]
        hidden = geglu(gate_val, up_val).astype(bf16)
        return gate_val, up_val, hidden, matmul_nt(hidden, w_down).astype(bf16)

    far_kept = forward(ffn_in[1])
    far_sum = over_cores(far_kept[3]).astype(bf16)
    near_in, far_sum = lax.optimization_barrier((ffn_in[0], far_sum))
    kept = (forward(near_in), far_kept)
    near_part, far_sum = lax.optimization_barrier((kept[0][3], swap(far_sum, "xh")))
    ffn_out = over_cores(near_part) + far_sum.astype(f32)
    mixed = (resid + rms_scale(ffn_out, gains[:, 3])).astype(bf16)
    grad_ffn_out, gain_three = norm_back(ffn_out, gains[:, 3], upstream)
    grad_own = grad_ffn_out.astype(bf16)
    grad_far = swap(grad_own, "xh")
    grad_near = jnp.concatenate([grad_own, swap(grad_own, "c")], axis=0)

    def backward(rows_in, gate_val, up_val):
        unused_value, pull = jax.vjp(geglu, gate_val, up_val)
        grad_gate, grad_up = pull(matmul(rows_in, w_down))
        return jnp.concatenate([grad_gate.astype(bf16), grad_up.astype(bf16)], axis=1)

    near_pulled = backward(grad_near, kept[0][0], kept[0][1])
    near_pulled, grad_far = lax.optimization_barrier((near_pulled, grad_far))
    grad_ffn = (grad_near, jnp.concatenate([grad_far, swap(grad_far, "c")], axis=0))
    far_pulled = backward(grad_ffn[1], kept[1][0], kept[1][1])
    far_sum = over_cores(matmul_nt(far_pulled, w_gate_up).astype(bf16)).astype(bf16)
    near_pulled, far_pulled, far_sum = lax.optimization_barrier(
        (near_pulled, far_pulled, far_sum)
    )
    grad_w = weight_sums(
        ffn_in, (near_pulled, far_pulled), grad_ffn, tuple(k[2] for k in kept)
    )
    grad_w, far_sum = lax.optimization_barrier((grad_w, swap(far_sum, "xh")))
    near_part = matmul_nt(near_pulled, w_gate_up).astype(bf16)
    grad_ffn_in = over_cores(near_part) + far_sum.astype(f32)

    ffn_rows = lax.psum_scatter(
        grad_w.reshape(NZ * NY, NXL * dp_rows, 3 * wide), ZY, scatter_dimension=0, tiled=False
    )
    ffn_rows = lax.optimization_barrier(ffn_rows)

    grad_from_ffn, gain_two = norm_back(resid, gains[:, 2], grad_ffn_in)
    grad_resid = upstream + grad_from_ffn
    grad_attn_out, gain_one = norm_back(attn_out, gains[:, 1], grad_resid)
    grad_attn = grad_attn_out.astype(bf16)

    grad_attn = matmul(grad_attn, to_attn).astype(bf16)

    def chip_sums(left, rights):
        sums = [matmul_tn(left, r).astype(bf16) for r in rights]
        half = len(sums) // 2
        return [
            (mine.astype(f32) + swap(sent, "c").astype(f32)).astype(bf16)
            for mine, sent in zip(sums[:half], sums[half:])
        ]

    out_near, out_far = chip_sums(grad_attn, attended)

    grad_attended = jnp.concatenate([matmul(grad_attn, w).astype(bf16) for w in w_out], axis=0)
    grad_value_all = matmul_tn(probs, grad_attended)
    grad_probs = matmul_nt(grad_attended, value_all)
    inner = jnp.sum(probs_full * grad_probs, axis=1, keepdims=True)
    grad_scores = (probs_full * (grad_probs - inner)).astype(bf16)
    grad_scores, out_near, out_far = lax.optimization_barrier((grad_scores, out_near, out_far))
    out_sum = from_x(out_near, out_far)
    grad_query_rot = (matmul(grad_scores, key_all) * score_scale).reshape(heads, rows, head_dim)
    grad_key_all = matmul_tn(grad_scores, query_flat) * score_scale
    grad_query_norm = rotate(grad_query_rot, cosine, -sine_table)
    grad_query_raw, gain_query = norm_back(query_raw, head_gains[:, 0], grad_query_norm)
    grad_query = grad_query_raw.astype(bf16)
    key_grads = jnp.concatenate([grad_key_all, grad_value_all], axis=1)
    query_sum = from_x(*chip_sums(normed, grad_query))
    own_grads = key_grads[back * rows :]
    key_low = key_grads[: back * rows].astype(bf16)
    for by in range(1, back + 1):
        part = key_low[(back - by) * rows : (back - by + 1) * rows]
        own_grads = own_grads + shifted(part, -by).astype(f32)
    grad_key_norm = rotate(own_grads[:, :head_dim], cosine, -sine_table)
    grad_key_raw, gain_key = norm_back(key_raw, head_gains[:, 1], grad_key_norm)
    grad_key = grad_key_raw.astype(bf16)
    grad_value = own_grads[:, head_dim:].astype(bf16)
    grad_kv_a = jnp.where(c == 0, grad_key, grad_value)
    grad_kv_b = jnp.where(c == 0, grad_value, grad_key)
    grad_normed = sum(matmul_nt(g, w) for g, w in zip(grad_query, w_query))
    grad_normed = grad_normed + matmul_nt(grad_kv_a, kv_a) + matmul_nt(grad_kv_b, kv_b)
    grad_from_norm, gain_zero = norm_back(inputs_a, gains_a[:, 0], grad_normed)
    tokens_grad = (exact(grad_resid, order) + exact(grad_from_norm, order_a)).astype(bf16)

    late_gains = jnp.stack([jnp.sum(g, axis=0) for g in (gain_one, gain_two, gain_three)], axis=0)
    late_gains = lax.dot(late_gains, to_attn.astype(f32), precision=lax.Precision.HIGHEST)
    norm_part = jnp.concatenate([jnp.sum(gain_zero, axis=0)[None], late_gains], axis=0).T
    head_part = jnp.stack([jnp.sum(gain_query, axis=(0, 1)), jnp.sum(gain_key, axis=0)], axis=1)
    head_cut = jnp.stack(sides(head_part.reshape(NZ * NXL * NY, -1)), axis=0)
    per_dp = head_cut.shape[-1]
    head_column = jnp.pad(head_cut, ((0, 0), (0, 0), (0, 0), (0, dp_rows - per_dp)))
    gain_cols = jnp.concatenate([norm_part, head_column.reshape(dim, 1)], axis=1)
    n_gain = gain_cols.shape[1]
    gain_cols = jnp.pad(gain_cols, ((0, 0), (0, 128 - n_gain))).astype(bf16)

    own = dim // 2

    def over_xl(chip):
        return (chip[:own].astype(f32) + swap(chip[own:], "xl").astype(f32)).astype(bf16)

    kv_sum = over_xl(chip_sums(normed, (grad_kv_a, grad_kv_b))[0])
    gain_sum = over_xl((gain_cols.astype(f32) + swap(gain_cols, "c").astype(f32)).astype(bf16))
    late = summed(jnp.concatenate([query_sum, out_sum, kv_sum, gain_sum], axis=1))
    mixed_out = matmul_nt(mixed, order).astype(bf16)
    late, ffn_rows, mixed_out, tokens_grad = lax.optimization_barrier(
        (late, ffn_rows, mixed_out, tokens_grad)
    )
    qo_share = late[:, : 2 * head_dim].reshape(dp_rows, 2, head_dim)
    x_sum = late[:, 2 * head_dim :].astype(bf16)
    x_sum = x_sum.astype(f32) + swap(x_sum, "xh").astype(f32)
    kv_mine = x_sum[:, :head_dim]
    kv_other = swap(kv_mine.astype(bf16), "c").astype(f32)
    kv_mine = kv_mine.astype(bf16).astype(f32)
    kv_total = jnp.concatenate(
        [jnp.where(c == 0, kv_mine, kv_other), jnp.where(c == 0, kv_other, kv_mine)], axis=1
    )
    norm_total = x_sum[:, head_dim : head_dim + 4]
    head_total = x_sum[:per_dp, head_dim + 4].reshape(-1, 2)

    ffn_share = ffn_rows[:dp_rows].astype(f32) + swap(ffn_rows[dp_rows:], "xl").astype(f32)
    ffn_share = ffn_share.reshape(dp_rows, 3, wide)[:, :, :ff]

    return (
        mixed_out,
        tokens_grad,
        norm_total,
        head_total,
        qo_share,
        kv_total,
        ffn_share,
    )


def solution(mesh):
    fine = Mesh(np.asarray(mesh.devices).reshape(NZ, NXL, NY, NXH, NC), ALL)
    dp, tensor = ("z", "xl", "y"), ("xh", "c")
    return jax.shard_map(
        body,
        mesh=fine,
        in_specs=(
            P(ALL, None),
            P(),
            P(),
            P(),
            P(dp, None, tensor),
            P(dp, None),
            P(dp, None, tensor),
            P(ALL, None),
        ),
        out_specs=(
            P(ALL, None),
            P(ALL, None),
            P(dp, None),
            P(dp, None),
            P(dp, None, tensor),
            P(dp, None),
            P(dp, None, tensor),
        ),
        check_vma=False,
    )
```

```python
import jax
import jax.numpy as jnp
import numpy as np
from jax import lax
from jax.experimental import pallas as pl
from jax.experimental.pallas import tpu as pltpu
from jax.sharding import Mesh
from jax.sharding import PartitionSpec as P

WINDOW = 512
NZ, NXL, NY, NXH, NC = 4, 2, 4, 2, 2
ALL = ("z", "xl", "y", "xh", "c")
ZY = ("z", "y")
BLOCKS = NZ * NXL * NY * NXH * NC

epsilon = 1e-06
rope_base = 10000.0
masked_score = -1e30
bf16 = jnp.bfloat16
f32 = jnp.float32


def rms_scale(values, gains):
    mean_square = jnp.mean(values * values, axis=-1, keepdims=True)
    return values * lax.rsqrt(mean_square + epsilon) * (1.0 + gains)


def norm_back(values, gains, upstream):
    inverse = lax.rsqrt(jnp.mean(values * values, axis=-1, keepdims=True) + epsilon)
    normed = values * inverse
    scaled = upstream * (1.0 + gains)
    grad_values = inverse * (scaled - normed * jnp.mean(scaled * normed, axis=-1, keepdims=True))
    return (grad_values, upstream * normed)


def rotate(values, cosine, sine_table):
    half_dim = values.shape[-1] // 2
    front = values[..., :half_dim]
    back_half = values[..., half_dim:]
    return jnp.concatenate(
        [front * cosine - back_half * sine_table, back_half * cosine + front * sine_table], axis=-1
    )


def rope_tables(position, head_dim):
    half_dim = head_dim // 2
    exponent = jnp.arange(half_dim).astype(f32) * (-2.0 / head_dim)
    frequency = jnp.power(f32(rope_base), exponent)
    angle = position.astype(f32)[:, None] * frequency[None, :]
    return (jnp.cos(angle), jnp.sin(angle))


def document_of(doc_lengths, index):
    ends = jnp.cumsum(doc_lengths)
    starts = ends - doc_lengths
    doc_number = jnp.sum((ends[None, :] <= index[:, None]).astype(jnp.int32), axis=1)
    owner = doc_number[:, None] == jnp.arange(doc_lengths.shape[0], dtype=jnp.int32)[None, :]
    position = index - jnp.sum(jnp.where(owner, starts[None, :], 0), axis=1)
    return (doc_number, position)


def geglu(gate_in, up_in):
    return jax.nn.gelu(gate_in, approximate=True) * up_in


def matmul(left, right):
    return jnp.dot(left, right, preferred_element_type=f32)


def matmul_nt(left, right):
    return lax.dot_general(left, right, (((1,), (1,)), ((), ())), preferred_element_type=f32)


def matmul_tn(left, right):
    return lax.dot_general(left, right, (((0,), (0,)), ((), ())), preferred_element_type=f32)


def swap(array, axis):
    return lax.ppermute(array, axis, [(0, 1), (1, 0)])


def swap_both(array):
    return lax.ppermute(array, ("xl", "xh"), [(0, 3), (1, 2), (2, 1), (3, 0)])


def shifted(array, by):
    return lax.ppermute(
        array, ALL, [(i, i + by) for i in range(BLOCKS) if 0 <= i + by < BLOCKS]
    )


def gathered(own):
    blocks = jnp.broadcast_to(own[None], (NZ * NY, *own.shape))
    return lax.all_to_all(blocks, ZY, 0, 0, tiled=True).reshape(-1, own.shape[1])


def summed(whole):
    blocks = whole.reshape(NZ * NY, -1, whole.shape[1])
    arrived = lax.all_to_all(blocks, ZY, 0, 0, tiled=True)
    return jnp.sum(arrived.astype(f32), axis=0)


def from_x(near, far):
    own = near.shape[0] // 2
    return (
        near[:own].astype(f32)
        + swap(near[own:], "xl").astype(f32)
        + swap(far[:own], "xh").astype(f32)
        + swap_both(far[own:]).astype(f32)
    ).astype(bf16)


def exact(left, right):
    return lax.dot_general(
        left, right.astype(f32), (((1,), (1,)), ((), ())), precision=lax.Precision.HIGH
    )


def weight_sums(ffn_in, grads, grad_out, hidden):
    rows, dim = ffn_in[0].shape
    width = hidden[0].shape[1] // 2
    first = grads[0].shape[1] // width

    def kernel(in_near, in_far, out_near, out_far, g_near, g_far, h_near, h_far, sums):
        def both(left, right):
            sums[...] = sum(matmul_tn(a[...], b[...]) for a, b in zip(left, right)).astype(bf16)

        @pl.when(pl.program_id(0) < first)
        def _():
            both((in_near, in_far), (g_near, g_far))

        @pl.when(pl.program_id(0) >= first)
        def _():
            both((out_near, out_far), (h_near, h_far))

    whole = pl.BlockSpec((rows, dim), lambda i: (0, 0))
    grad_tile = pl.BlockSpec((rows, width), lambda i: (0, jnp.minimum(i, first - 1)))
    hidden_tile = pl.BlockSpec((rows, width), lambda i: (0, jnp.maximum(i - first, 0)))
    return pl.pallas_call(
        kernel,
        grid=(first + 2,),
        out_shape=jax.ShapeDtypeStruct((dim, (first + 2) * width), bf16),
        in_specs=[whole] * 4 + [grad_tile] * 2 + [hidden_tile] * 2,
        out_specs=pl.BlockSpec((dim, width), lambda i: (0, i)),
        compiler_params=pltpu.CompilerParams(vmem_limit_bytes=40 * 2**20),
        cost_estimate=pl.CostEstimate(
            flops=4 * rows * dim * (first + 2) * width,
            bytes_accessed=2 * (first + 2) * width * (dim + 2 * rows),
            transcendentals=0,
        ),
    )(*ffn_in, *grad_out, *grads, *hidden)


def over_cores(part):
    own = part.shape[0] // 2
    return part[:own].astype(f32) + swap(part[own:], "c").astype(f32)


def group_rows(own):
    far = swap(own, "xh")
    return (
        jnp.concatenate([own, swap(own, "c")], axis=0),
        jnp.concatenate([far, swap(far, "c")], axis=0),
    )


def body(tokens, doc_lengths, norm_gains, head_gains, q_o, kv_weight, ffn_weight, out_grad):
    rows = tokens.shape[0]
    dim = tokens.shape[1]
    head_dim = head_gains.shape[0]
    score_scale = head_dim ** (-0.5)
    xl = lax.axis_index("xl")
    c = lax.axis_index("c")
    dp_rows = q_o.shape[0]
    ff = ffn_weight.shape[2]
    ff_pad = -ff % 256
    wide = ff + ff_pad

    kv_half = lax.dynamic_slice_in_dim(kv_weight, c * head_dim, head_dim, 1)
    small = jnp.concatenate([q_o[:, 0, :], kv_half, q_o[:, 1, :]], axis=1)
    ffn_own = jnp.pad(ffn_weight, ((0, 0), (0, 0), (0, ff_pad))).reshape(dp_rows, 3 * wide)
    ffn_other = swap(ffn_own, "xl")
    ffn_pair = jnp.concatenate([ffn_own, ffn_other], axis=0)
    quarter = gathered(small)
    q_own, kv_own, o_own = (quarter[:, k * head_dim : (k + 1) * head_dim] for k in range(3))

    def rows_of(own, other):
        return jnp.concatenate([own, other], axis=0)

    kv_a = rows_of(kv_own, swap(kv_own, "xl"))
    kv_b = swap(kv_a, "c")
    q_rest = (swap(q_own, "xl"), swap(q_own, "xh"), swap_both(q_own))
    ffn_full = lax.all_gather(ffn_pair, ZY, axis=0, tiled=True)

    place = jnp.arange(dim, dtype=jnp.int32)
    row = place % dp_rows

    def one_hot(source):
        return (place[:, None] == source[None, :]).astype(bf16)

    def source(z_of, y_of, side):
        return ((z_of * NXL + jnp.bitwise_xor(side, xl)) * NY + y_of) * dp_rows + row

    step = place // dp_rows
    order = one_hot(source(step // (NXL * NY), (step // NXL) % NY, step % NXL))
    order_a = one_hot(source((step // NY) % NZ, step % NY, step // (NZ * NY)))
    to_attn = one_hot(((step % (NZ * NY)) * NXL + step // (NZ * NY)) * dp_rows + row)

    def sides(array):
        cut = array.reshape(NZ, NXL, NY, *array.shape[1:])
        first = jnp.where(xl == 0, cut[:, 0], cut[:, 1])
        second = jnp.where(xl == 0, cut[:, 1], cut[:, 0])
        return first, second

    gain_sides = sides(norm_gains.reshape(NZ * NXL * NY, dp_rows, -1))
    gains = jnp.stack(gain_sides, axis=2).reshape(norm_gains.shape)
    gains_a = jnp.stack(gain_sides, axis=0).reshape(norm_gains.shape)
    inputs = matmul(tokens, order)
    inputs_a = matmul(tokens, order_a)
    upstream = matmul(out_grad, order)
    inputs, inputs_a, upstream = lax.optimization_barrier((inputs, inputs_a, upstream))

    block = ((lax.axis_index("z") * NXL + xl) * NY + lax.axis_index("y")) * NXH * NC
    block = block + lax.axis_index("xh") * NC + c
    back = WINDOW // rows
    key_index = (block - back) * rows + jnp.arange((back + 1) * rows, dtype=jnp.int32)
    key_doc, key_position = document_of(doc_lengths, key_index)
    key_doc = jnp.where(key_index < 0, -1, key_doc)
    query_index = key_index[back * rows :]
    query_doc = key_doc[back * rows :]
    cosine, sine_table = rope_tables(key_position[back * rows :], head_dim)
    distance = query_index[:, None] - key_index[None, :]
    allowed = (query_doc[:, None] == key_doc[None, :]) & (distance >= 0) & (distance < WINDOW)

    normed = rms_scale(inputs_a, gains_a[:, 0]).astype(bf16)
    from_a, from_b = matmul(normed, kv_a), matmul(normed, kv_b)
    key_raw = jnp.where(c == 0, from_a, from_b)
    value_low = jnp.where(c == 0, from_b, from_a).astype(bf16)
    key_rot = rotate(rms_scale(key_raw, head_gains[:, 1]), cosine, sine_table).astype(bf16)
    packed = jnp.concatenate([key_rot, value_low], axis=1)
    q_rest, o_own = lax.optimization_barrier((q_rest, o_own))
    o_rest = (swap(o_own, "xl"), swap(o_own, "xh"), swap_both(o_own))
    earlier = tuple(shifted(packed, by) for by in range(back, 0, -1))
    q_rest, earlier = lax.optimization_barrier((q_rest, earlier))
    q_near, q_far = rows_of(q_own, q_rest[0]), rows_of(q_rest[1], q_rest[2])
    both = jnp.concatenate([*earlier, packed], axis=0)
    key_all, value_all = both[:, :head_dim], both[:, head_dim:]
    w_query = (q_near, q_far, swap(q_near, "c"), swap(q_far, "c"))
    query_raw = jnp.stack([matmul(normed, w) for w in w_query], axis=0)
    query_rot = rotate(rms_scale(query_raw, head_gains[:, 0]), cosine, sine_table).astype(bf16)
    heads = query_raw.shape[0]
    query_flat = query_rot.reshape(heads * rows, head_dim)
    scores = matmul_nt(query_flat, key_all).reshape(heads, rows, -1) * score_scale
    scores = jnp.where(allowed[None], scores, masked_score)
    top_score = jnp.max(scores, axis=2, keepdims=True)
    weights = jnp.exp(scores - top_score)
    total = jnp.sum(weights, axis=2, keepdims=True)
    probs_full = (weights / total).reshape(heads * rows, -1)
    probs = probs_full.astype(bf16)
    attended = matmul(probs, value_all).astype(bf16).reshape(heads, rows, head_dim)
    attended, o_rest = lax.optimization_barrier((attended, o_rest))
    o_near, o_far = rows_of(o_own, o_rest[0]), rows_of(o_rest[1], o_rest[2])
    w_out = (o_near, o_far, swap(o_near, "c"), swap(o_far, "c"))
    attn_out = exact(sum(matmul_nt(a, w) for a, w in zip(attended, w_out)), to_attn)
    resid = inputs + rms_scale(attn_out, gains[:, 1])

    ffn_in = group_rows(rms_scale(resid, gains[:, 2]).astype(bf16))
    w_gate_up, w_down = ffn_full[:, : 2 * wide], ffn_full[:, 2 * wide :]

    def forward(rows_in):
        gate_up = matmul(rows_in, w_gate_up)
        gate_val, up_val = gate_up[:, :wide], gate_up[:, wide:]
        hidden = geglu(gate_val, up_val).astype(bf16)
        return gate_val, up_val, hidden, matmul_nt(hidden, w_down).astype(bf16)

    far_kept = forward(ffn_in[1])
    far_sum = over_cores(far_kept[3]).astype(bf16)
    near_in, far_sum = lax.optimization_barrier((ffn_in[0], far_sum))
    kept = (forward(near_in), far_kept)
    near_part, far_sum = lax.optimization_barrier((kept[0][3], swap(far_sum, "xh")))
    ffn_out = over_cores(near_part) + far_sum.astype(f32)
    mixed = (resid + rms_scale(ffn_out, gains[:, 3])).astype(bf16)
    grad_ffn_out, gain_three = norm_back(ffn_out, gains[:, 3], upstream)
    grad_own = grad_ffn_out.astype(bf16)
    grad_far = swap(grad_own, "xh")
    grad_near = jnp.concatenate([grad_own, swap(grad_own, "c")], axis=0)

    def backward(rows_in, gate_val, up_val):
        unused_value, pull = jax.vjp(geglu, gate_val, up_val)
        grad_gate, grad_up = pull(matmul(rows_in, w_down))
        return jnp.concatenate([grad_gate.astype(bf16), grad_up.astype(bf16)], axis=1)

    near_pulled = backward(grad_near, kept[0][0], kept[0][1])
    near_pulled, grad_far = lax.optimization_barrier((near_pulled, grad_far))
    grad_ffn = (grad_near, jnp.concatenate([grad_far, swap(grad_far, "c")], axis=0))
    far_pulled = backward(grad_ffn[1], kept[1][0], kept[1][1])
    far_sum = over_cores(matmul_nt(far_pulled, w_gate_up).astype(bf16)).astype(bf16)
    near_pulled, far_pulled, far_sum = lax.optimization_barrier(
        (near_pulled, far_pulled, far_sum)
    )
    grad_w = weight_sums(
        ffn_in, (near_pulled, far_pulled), grad_ffn, tuple(k[2] for k in kept)
    )
    grad_w, far_sum = lax.optimization_barrier((grad_w, swap(far_sum, "xh")))
    near_part = matmul_nt(near_pulled, w_gate_up).astype(bf16)
    grad_ffn_in = over_cores(near_part) + far_sum.astype(f32)

    ffn_rows = lax.psum_scatter(
        grad_w.reshape(NZ * NY, NXL * dp_rows, 3 * wide), ZY, scatter_dimension=0, tiled=False
    )
    ffn_rows = lax.optimization_barrier(ffn_rows)

    grad_from_ffn, gain_two = norm_back(resid, gains[:, 2], grad_ffn_in)
    grad_resid = upstream + grad_from_ffn
    grad_attn_out, gain_one = norm_back(attn_out, gains[:, 1], grad_resid)
    grad_attn = grad_attn_out.astype(bf16)

    grad_attn = matmul(grad_attn, to_attn).astype(bf16)

    def chip_sums(left, rights):
        sums = [matmul_tn(left, r).astype(bf16) for r in rights]
        half = len(sums) // 2
        return [
            (mine.astype(f32) + swap(sent, "c").astype(f32)).astype(bf16)
            for mine, sent in zip(sums[:half], sums[half:])
        ]

    out_near, out_far = chip_sums(grad_attn, attended)

    grad_attended = jnp.concatenate([matmul(grad_attn, w).astype(bf16) for w in w_out], axis=0)
    grad_value_all = matmul_tn(probs, grad_attended)
    grad_probs = matmul_nt(grad_attended, value_all)
    inner = jnp.sum(probs_full * grad_probs, axis=1, keepdims=True)
    grad_scores = (probs_full * (grad_probs - inner)).astype(bf16)
    grad_scores, out_near, out_far = lax.optimization_barrier((grad_scores, out_near, out_far))
    out_sum = from_x(out_near, out_far)
    grad_query_rot = (matmul(grad_scores, key_all) * score_scale).reshape(heads, rows, head_dim)
    grad_key_all = matmul_tn(grad_scores, query_flat) * score_scale
    grad_query_norm = rotate(grad_query_rot, cosine, -sine_table)
    grad_query_raw, gain_query = norm_back(query_raw, head_gains[:, 0], grad_query_norm)
    grad_query = grad_query_raw.astype(bf16)
    key_grads = jnp.concatenate([grad_key_all, grad_value_all], axis=1)
    query_sum = from_x(*chip_sums(normed, grad_query))
    own_grads = key_grads[back * rows :]
    key_low = key_grads[: back * rows].astype(bf16)
    for by in range(1, back + 1):
        part = key_low[(back - by) * rows : (back - by + 1) * rows]
        own_grads = own_grads + shifted(part, -by).astype(f32)
    grad_key_norm = rotate(own_grads[:, :head_dim], cosine, -sine_table)
    grad_key_raw, gain_key = norm_back(key_raw, head_gains[:, 1], grad_key_norm)
    grad_key = grad_key_raw.astype(bf16)
    grad_value = own_grads[:, head_dim:].astype(bf16)
    grad_kv_a = jnp.where(c == 0, grad_key, grad_value)
    grad_kv_b = jnp.where(c == 0, grad_value, grad_key)
    grad_normed = sum(matmul_nt(g, w) for g, w in zip(grad_query, w_query))
    grad_normed = grad_normed + matmul_nt(grad_kv_a, kv_a) + matmul_nt(grad_kv_b, kv_b)
    grad_from_norm, gain_zero = norm_back(inputs_a, gains_a[:, 0], grad_normed)
    tokens_grad = (exact(grad_resid, order) + exact(grad_from_norm, order_a)).astype(bf16)

    late_gains = jnp.stack([jnp.sum(g, axis=0) for g in (gain_one, gain_two, gain_three)], axis=0)
    late_gains = lax.dot(late_gains, to_attn.astype(f32), precision=lax.Precision.HIGHEST)
    norm_part = jnp.concatenate([jnp.sum(gain_zero, axis=0)[None], late_gains], axis=0).T
    head_part = jnp.stack([jnp.sum(gain_query, axis=(0, 1)), jnp.sum(gain_key, axis=0)], axis=1)
    head_cut = jnp.stack(sides(head_part.reshape(NZ * NXL * NY, -1)), axis=0)
    per_dp = head_cut.shape[-1]
    head_column = jnp.pad(head_cut, ((0, 0), (0, 0), (0, 0), (0, dp_rows - per_dp)))
    gain_cols = jnp.concatenate([norm_part, head_column.reshape(dim, 1)], axis=1)
    n_gain = gain_cols.shape[1]
    gain_cols = jnp.pad(gain_cols, ((0, 0), (0, 128 - n_gain))).astype(bf16)

    own = dim // 2

    def over_xl(chip):
        return (chip[:own].astype(f32) + swap(chip[own:], "xl").astype(f32)).astype(bf16)

    kv_sum = over_xl(chip_sums(normed, (grad_kv_a, grad_kv_b))[0])
    gain_sum = over_xl((gain_cols.astype(f32) + swap(gain_cols, "c").astype(f32)).astype(bf16))
    late = summed(jnp.concatenate([query_sum, out_sum, kv_sum, gain_sum], axis=1))
    mixed_out = matmul_nt(mixed, order).astype(bf16)
    late, near, far, mixed_out, tokens_grad = lax.optimization_barrier(
        (late, ffn_rows[:dp_rows], ffn_rows[dp_rows:], mixed_out, tokens_grad)
    )
    qo_share = late[:, : 2 * head_dim].reshape(dp_rows, 2, head_dim)
    x_sum = late[:, 2 * head_dim :].astype(bf16)
    x_sum = x_sum.astype(f32) + swap(x_sum, "xh").astype(f32)
    kv_mine = x_sum[:, :head_dim]
    kv_other = swap(kv_mine.astype(bf16), "c").astype(f32)
    kv_mine = kv_mine.astype(bf16).astype(f32)
    kv_total = jnp.concatenate(
        [jnp.where(c == 0, kv_mine, kv_other), jnp.where(c == 0, kv_other, kv_mine)], axis=1
    )
    norm_total = x_sum[:, head_dim : head_dim + 4]
    head_total = x_sum[:per_dp, head_dim + 4].reshape(-1, 2)

    ffn_share = near.astype(f32) + swap(far, "xl").astype(f32)
    ffn_share = ffn_share.reshape(dp_rows, 3, wide)[:, :, :ff]

    return (
        mixed_out,
        tokens_grad,
        norm_total,
        head_total,
        qo_share,
        kv_total,
        ffn_share,
    )


def solution(mesh):
    fine = Mesh(np.asarray(mesh.devices).reshape(NZ, NXL, NY, NXH, NC), ALL)
    dp, tensor = ("z", "xl", "y"), ("xh", "c")
    return jax.shard_map(
        body,
        mesh=fine,
        in_specs=(
            P(ALL, None),
            P(),
            P(),
            P(),
            P(dp, None, tensor),
            P(dp, None),
            P(dp, None, tensor),
            P(ALL, None),
        ),
        out_specs=(
            P(ALL, None),
            P(ALL, None),
            P(dp, None),
            P(dp, None),
            P(dp, None, tensor),
            P(dp, None),
            P(dp, None, tensor),
        ),
        check_vma=False,
    )
```

```python
import jax
import jax.numpy as jnp
import numpy as np
from jax import lax
from jax.experimental import pallas as pl
from jax.experimental.pallas import tpu as pltpu
from jax.sharding import Mesh
from jax.sharding import PartitionSpec as P

WINDOW = 512
NZ, NXL, NY, NXH, NC = 4, 2, 4, 2, 2
ALL = ("z", "xl", "y", "xh", "c")
ZY = ("z", "y")
BLOCKS = NZ * NXL * NY * NXH * NC

epsilon = 1e-06
rope_base = 10000.0
masked_score = -1e30
bf16 = jnp.bfloat16
f32 = jnp.float32


def rms_scale(values, gains):
    mean_square = jnp.mean(values * values, axis=-1, keepdims=True)
    return values * lax.rsqrt(mean_square + epsilon) * (1.0 + gains)


def norm_back(values, gains, upstream):
    inverse = lax.rsqrt(jnp.mean(values * values, axis=-1, keepdims=True) + epsilon)
    normed = values * inverse
    scaled = upstream * (1.0 + gains)
    grad_values = inverse * (scaled - normed * jnp.mean(scaled * normed, axis=-1, keepdims=True))
    return (grad_values, upstream * normed)


def rotate(values, cosine, sine_table):
    half_dim = values.shape[-1] // 2
    front = values[..., :half_dim]
    back_half = values[..., half_dim:]
    return jnp.concatenate(
        [front * cosine - back_half * sine_table, back_half * cosine + front * sine_table], axis=-1
    )


def rope_tables(position, head_dim):
    half_dim = head_dim // 2
    exponent = jnp.arange(half_dim).astype(f32) * (-2.0 / head_dim)
    frequency = jnp.power(f32(rope_base), exponent)
    angle = position.astype(f32)[:, None] * frequency[None, :]
    return (jnp.cos(angle), jnp.sin(angle))


def document_of(doc_lengths, index):
    ends = jnp.cumsum(doc_lengths)
    starts = ends - doc_lengths
    doc_number = jnp.sum((ends[None, :] <= index[:, None]).astype(jnp.int32), axis=1)
    owner = doc_number[:, None] == jnp.arange(doc_lengths.shape[0], dtype=jnp.int32)[None, :]
    position = index - jnp.sum(jnp.where(owner, starts[None, :], 0), axis=1)
    return (doc_number, position)


def geglu(gate_in, up_in):
    return jax.nn.gelu(gate_in, approximate=True) * up_in


def matmul(left, right):
    return jnp.dot(left, right, preferred_element_type=f32)


def matmul_nt(left, right):
    return lax.dot_general(left, right, (((1,), (1,)), ((), ())), preferred_element_type=f32)


def matmul_tn(left, right):
    return lax.dot_general(left, right, (((0,), (0,)), ((), ())), preferred_element_type=f32)


def swap(array, axis):
    return lax.ppermute(array, axis, [(0, 1), (1, 0)])


def swap_both(array):
    return lax.ppermute(array, ("xl", "xh"), [(0, 3), (1, 2), (2, 1), (3, 0)])


def shifted(array, by):
    return lax.ppermute(
        array, ALL, [(i, i + by) for i in range(BLOCKS) if 0 <= i + by < BLOCKS]
    )


def gathered(own):
    blocks = jnp.broadcast_to(own[None], (NZ * NY, *own.shape))
    return lax.all_to_all(blocks, ZY, 0, 0, tiled=True).reshape(-1, own.shape[1])


def summed(whole):
    blocks = whole.reshape(NZ * NY, -1, whole.shape[1])
    arrived = lax.all_to_all(blocks, ZY, 0, 0, tiled=True)
    return jnp.sum(arrived.astype(f32), axis=0)


def from_x(near, far):
    own = near.shape[0] // 2
    return (
        near[:own].astype(f32)
        + swap(near[own:], "xl").astype(f32)
        + swap(far[:own], "xh").astype(f32)
        + swap_both(far[own:]).astype(f32)
    ).astype(bf16)


def exact(left, right):
    return lax.dot_general(
        left, right.astype(f32), (((1,), (1,)), ((), ())), precision=lax.Precision.HIGH
    )


def weight_sums(ffn_in, grads, grad_out, hidden):
    rows, dim = ffn_in[0].shape
    width = hidden[0].shape[1]
    first = grads[0].shape[1] // width
    chunk = dim // 3

    def kernel(in_near, in_far, out_near, out_far, g_near, g_far, h_near, h_far, sums):
        def product(lefts, rights):
            right = jnp.concatenate([r[...] for r in rights], axis=0)
            for at in range(0, dim, chunk):
                left = jnp.concatenate([part[:, at : at + chunk] for part in lefts], axis=0)
                sums[at : at + chunk, :] = matmul_tn(left, right).astype(bf16)

        @pl.when(pl.program_id(0) < first)
        def _():
            product((in_near, in_far), (g_near, g_far))

        @pl.when(pl.program_id(0) >= first)
        def _():
            product((out_near, out_far), (h_near, h_far))

    whole = pl.BlockSpec((rows, dim), lambda i: (0, 0))
    grad_tile = pl.BlockSpec((rows, width), lambda i: (0, jnp.minimum(i, first - 1)))
    hidden_tile = pl.BlockSpec((rows, width), lambda i: (0, 0))
    return pl.pallas_call(
        kernel,
        grid=(first + 1,),
        out_shape=jax.ShapeDtypeStruct((dim, (first + 1) * width), bf16),
        in_specs=[whole] * 4 + [grad_tile] * 2 + [hidden_tile] * 2,
        out_specs=pl.BlockSpec((dim, width), lambda i: (0, i)),
        compiler_params=pltpu.CompilerParams(vmem_limit_bytes=40 * 2**20),
        cost_estimate=pl.CostEstimate(
            flops=4 * rows * dim * (first + 1) * width,
            bytes_accessed=2 * (first + 1) * width * (dim + 2 * rows),
            transcendentals=0,
        ),
    )(*ffn_in, *grad_out, *grads, *hidden)


def over_cores(part):
    own = part.shape[0] // 2
    return part[:own].astype(f32) + swap(part[own:], "c").astype(f32)


def group_rows(own):
    far = swap(own, "xh")
    return (
        jnp.concatenate([own, swap(own, "c")], axis=0),
        jnp.concatenate([far, swap(far, "c")], axis=0),
    )


def body(tokens, doc_lengths, norm_gains, head_gains, q_o, kv_weight, ffn_weight, out_grad):
    rows = tokens.shape[0]
    dim = tokens.shape[1]
    head_dim = head_gains.shape[0]
    score_scale = head_dim ** (-0.5)
    xl = lax.axis_index("xl")
    c = lax.axis_index("c")
    dp_rows = q_o.shape[0]
    ff = ffn_weight.shape[2]
    ff_pad = -ff % 256
    wide = ff + ff_pad

    kv_half = lax.dynamic_slice_in_dim(kv_weight, c * head_dim, head_dim, 1)
    small = jnp.concatenate([q_o[:, 0, :], kv_half, q_o[:, 1, :]], axis=1)
    ffn_own = jnp.pad(ffn_weight, ((0, 0), (0, 0), (0, ff_pad))).reshape(dp_rows, 3 * wide)
    ffn_other = swap(ffn_own, "xl")
    ffn_pair = jnp.concatenate([ffn_own, ffn_other], axis=0)
    quarter = gathered(small)
    q_own, kv_own, o_own = (quarter[:, k * head_dim : (k + 1) * head_dim] for k in range(3))

    def rows_of(own, other):
        return jnp.concatenate([own, other], axis=0)

    kv_a = rows_of(kv_own, swap(kv_own, "xl"))
    kv_b = swap(kv_a, "c")
    q_rest = (swap(q_own, "xl"), swap(q_own, "xh"), swap_both(q_own))
    ffn_full = lax.all_gather(ffn_pair, ZY, axis=0, tiled=True)

    place = jnp.arange(dim, dtype=jnp.int32)
    row = place % dp_rows

    def one_hot(source):
        return (place[:, None] == source[None, :]).astype(bf16)

    def source(z_of, y_of, side):
        return ((z_of * NXL + jnp.bitwise_xor(side, xl)) * NY + y_of) * dp_rows + row

    step = place // dp_rows
    order = one_hot(source(step // (NXL * NY), (step // NXL) % NY, step % NXL))
    order_a = one_hot(source((step // NY) % NZ, step % NY, step // (NZ * NY)))
    to_attn = one_hot(((step % (NZ * NY)) * NXL + step // (NZ * NY)) * dp_rows + row)

    def sides(array):
        cut = array.reshape(NZ, NXL, NY, *array.shape[1:])
        first = jnp.where(xl == 0, cut[:, 0], cut[:, 1])
        second = jnp.where(xl == 0, cut[:, 1], cut[:, 0])
        return first, second

    gain_sides = sides(norm_gains.reshape(NZ * NXL * NY, dp_rows, -1))
    gains = jnp.stack(gain_sides, axis=2).reshape(norm_gains.shape)
    gains_a = jnp.stack(gain_sides, axis=0).reshape(norm_gains.shape)
    inputs = matmul(tokens, order)
    inputs_a = matmul(tokens, order_a)
    upstream = matmul(out_grad, order)
    inputs, inputs_a, upstream = lax.optimization_barrier((inputs, inputs_a, upstream))

    block = ((lax.axis_index("z") * NXL + xl) * NY + lax.axis_index("y")) * NXH * NC
    block = block + lax.axis_index("xh") * NC + c
    back = WINDOW // rows
    key_index = (block - back) * rows + jnp.arange((back + 1) * rows, dtype=jnp.int32)
    key_doc, key_position = document_of(doc_lengths, key_index)
    key_doc = jnp.where(key_index < 0, -1, key_doc)
    query_index = key_index[back * rows :]
    query_doc = key_doc[back * rows :]
    cosine, sine_table = rope_tables(key_position[back * rows :], head_dim)
    distance = query_index[:, None] - key_index[None, :]
    allowed = (query_doc[:, None] == key_doc[None, :]) & (distance >= 0) & (distance < WINDOW)

    normed = rms_scale(inputs_a, gains_a[:, 0]).astype(bf16)
    from_a, from_b = matmul(normed, kv_a), matmul(normed, kv_b)
    key_raw = jnp.where(c == 0, from_a, from_b)
    value_low = jnp.where(c == 0, from_b, from_a).astype(bf16)
    key_rot = rotate(rms_scale(key_raw, head_gains[:, 1]), cosine, sine_table).astype(bf16)
    packed = jnp.concatenate([key_rot, value_low], axis=1)
    q_rest, o_own = lax.optimization_barrier((q_rest, o_own))
    o_rest = (swap(o_own, "xl"), swap(o_own, "xh"), swap_both(o_own))
    earlier = tuple(shifted(packed, by) for by in range(back, 0, -1))
    q_rest, earlier = lax.optimization_barrier((q_rest, earlier))
    q_near, q_far = rows_of(q_own, q_rest[0]), rows_of(q_rest[1], q_rest[2])
    both = jnp.concatenate([*earlier, packed], axis=0)
    key_all, value_all = both[:, :head_dim], both[:, head_dim:]
    w_query = (q_near, q_far, swap(q_near, "c"), swap(q_far, "c"))
    query_raw = jnp.stack([matmul(normed, w) for w in w_query], axis=0)
    query_rot = rotate(rms_scale(query_raw, head_gains[:, 0]), cosine, sine_table).astype(bf16)
    heads = query_raw.shape[0]
    query_flat = query_rot.reshape(heads * rows, head_dim)
    scores = matmul_nt(query_flat, key_all).reshape(heads, rows, -1) * score_scale
    scores = jnp.where(allowed[None], scores, masked_score)
    top_score = jnp.max(scores, axis=2, keepdims=True)
    weights = jnp.exp(scores - top_score)
    total = jnp.sum(weights, axis=2, keepdims=True)
    probs_full = (weights / total).reshape(heads * rows, -1)
    probs = probs_full.astype(bf16)
    attended = matmul(probs, value_all).astype(bf16).reshape(heads, rows, head_dim)
    attended, o_rest = lax.optimization_barrier((attended, o_rest))
    o_near, o_far = rows_of(o_own, o_rest[0]), rows_of(o_rest[1], o_rest[2])
    w_out = (o_near, o_far, swap(o_near, "c"), swap(o_far, "c"))
    attn_out = exact(sum(matmul_nt(a, w) for a, w in zip(attended, w_out)), to_attn)
    resid = inputs + rms_scale(attn_out, gains[:, 1])

    ffn_in = group_rows(rms_scale(resid, gains[:, 2]).astype(bf16))
    w_gate_up, w_down = ffn_full[:, : 2 * wide], ffn_full[:, 2 * wide :]

    def forward(rows_in):
        gate_up = matmul(rows_in, w_gate_up)
        gate_val, up_val = gate_up[:, :wide], gate_up[:, wide:]
        hidden = geglu(gate_val, up_val).astype(bf16)
        return gate_val, up_val, hidden, matmul_nt(hidden, w_down).astype(bf16)

    ffn_in = lax.optimization_barrier(ffn_in)
    far_kept = forward(ffn_in[1])
    far_sum = over_cores(far_kept[3]).astype(bf16)
    near_in, far_sum = lax.optimization_barrier((ffn_in[0], far_sum))
    kept = (forward(near_in), far_kept)
    near_part, far_sum = lax.optimization_barrier((kept[0][3], swap(far_sum, "xh")))
    ffn_out = over_cores(near_part) + far_sum.astype(f32)
    mixed = (resid + rms_scale(ffn_out, gains[:, 3])).astype(bf16)
    grad_ffn_out, gain_three = norm_back(ffn_out, gains[:, 3], upstream)
    grad_own = grad_ffn_out.astype(bf16)
    grad_far = swap(grad_own, "xh")
    grad_near = jnp.concatenate([grad_own, swap(grad_own, "c")], axis=0)

    def backward(rows_in, gate_val, up_val):
        unused_value, pull = jax.vjp(geglu, gate_val, up_val)
        grad_gate, grad_up = pull(matmul(rows_in, w_down))
        return jnp.concatenate([grad_gate.astype(bf16), grad_up.astype(bf16)], axis=1)

    near_pulled = backward(grad_near, kept[0][0], kept[0][1])
    near_pulled, grad_far = lax.optimization_barrier((near_pulled, grad_far))
    grad_ffn = (grad_near, jnp.concatenate([grad_far, swap(grad_far, "c")], axis=0))
    far_pulled = backward(grad_ffn[1], kept[1][0], kept[1][1])
    far_sum = over_cores(matmul_nt(far_pulled, w_gate_up).astype(bf16)).astype(bf16)
    near_pulled, far_pulled, far_sum = lax.optimization_barrier(
        (near_pulled, far_pulled, far_sum)
    )
    grad_w = weight_sums(
        ffn_in, (near_pulled, far_pulled), grad_ffn, tuple(k[2] for k in kept)
    )
    grad_w, far_sum = lax.optimization_barrier((grad_w, swap(far_sum, "xh")))
    near_part = matmul_nt(near_pulled, w_gate_up).astype(bf16)
    grad_ffn_in = over_cores(near_part) + far_sum.astype(f32)

    ffn_rows = lax.psum_scatter(
        grad_w.reshape(NZ * NY, NXL * dp_rows, 3 * wide), ZY, scatter_dimension=0, tiled=False
    )
    ffn_rows = lax.optimization_barrier(ffn_rows)

    grad_from_ffn, gain_two = norm_back(resid, gains[:, 2], grad_ffn_in)
    grad_resid = upstream + grad_from_ffn
    grad_attn_out, gain_one = norm_back(attn_out, gains[:, 1], grad_resid)
    grad_attn = grad_attn_out.astype(bf16)

    grad_attn = matmul(grad_attn, to_attn).astype(bf16)

    def chip_sums(left, rights):
        sums = [matmul_tn(left, r).astype(bf16) for r in rights]
        half = len(sums) // 2
        return [
            (mine.astype(f32) + swap(sent, "c").astype(f32)).astype(bf16)
            for mine, sent in zip(sums[:half], sums[half:])
        ]

    out_near, out_far = chip_sums(grad_attn, attended)

    grad_attended = jnp.concatenate([matmul(grad_attn, w).astype(bf16) for w in w_out], axis=0)
    grad_value_all = matmul_tn(probs, grad_attended)
    grad_probs = matmul_nt(grad_attended, value_all)
    inner = jnp.sum(probs_full * grad_probs, axis=1, keepdims=True)
    grad_scores = (probs_full * (grad_probs - inner)).astype(bf16)
    grad_scores, out_near, out_far = lax.optimization_barrier((grad_scores, out_near, out_far))
    out_sum = from_x(out_near, out_far)
    grad_query_rot = (matmul(grad_scores, key_all) * score_scale).reshape(heads, rows, head_dim)
    grad_key_all = matmul_tn(grad_scores, query_flat) * score_scale
    grad_query_norm = rotate(grad_query_rot, cosine, -sine_table)
    grad_query_raw, gain_query = norm_back(query_raw, head_gains[:, 0], grad_query_norm)
    grad_query = grad_query_raw.astype(bf16)
    key_grads = jnp.concatenate([grad_key_all, grad_value_all], axis=1)
    query_sum = from_x(*chip_sums(normed, grad_query))
    own_grads = key_grads[back * rows :]
    key_low = key_grads[: back * rows].astype(bf16)
    for by in range(1, back + 1):
        part = key_low[(back - by) * rows : (back - by + 1) * rows]
        own_grads = own_grads + shifted(part, -by).astype(f32)
    grad_key_norm = rotate(own_grads[:, :head_dim], cosine, -sine_table)
    grad_key_raw, gain_key = norm_back(key_raw, head_gains[:, 1], grad_key_norm)
    grad_key = grad_key_raw.astype(bf16)
    grad_value = own_grads[:, head_dim:].astype(bf16)
    grad_kv_a = jnp.where(c == 0, grad_key, grad_value)
    grad_kv_b = jnp.where(c == 0, grad_value, grad_key)
    grad_normed = sum(matmul_nt(g, w) for g, w in zip(grad_query, w_query))
    grad_normed = grad_normed + matmul_nt(grad_kv_a, kv_a) + matmul_nt(grad_kv_b, kv_b)
    grad_from_norm, gain_zero = norm_back(inputs_a, gains_a[:, 0], grad_normed)
    tokens_grad = (exact(grad_resid, order) + exact(grad_from_norm, order_a)).astype(bf16)

    late_gains = jnp.stack([jnp.sum(g, axis=0) for g in (gain_one, gain_two, gain_three)], axis=0)
    late_gains = lax.dot(late_gains, to_attn.astype(f32), precision=lax.Precision.HIGHEST)
    norm_part = jnp.concatenate([jnp.sum(gain_zero, axis=0)[None], late_gains], axis=0).T
    head_part = jnp.stack([jnp.sum(gain_query, axis=(0, 1)), jnp.sum(gain_key, axis=0)], axis=1)
    head_cut = jnp.stack(sides(head_part.reshape(NZ * NXL * NY, -1)), axis=0)
    per_dp = head_cut.shape[-1]
    head_column = jnp.pad(head_cut, ((0, 0), (0, 0), (0, 0), (0, dp_rows - per_dp)))
    gain_cols = jnp.concatenate([norm_part, head_column.reshape(dim, 1)], axis=1)
    n_gain = gain_cols.shape[1]
    gain_cols = jnp.pad(gain_cols, ((0, 0), (0, 128 - n_gain))).astype(bf16)

    own = dim // 2

    def over_xl(chip):
        return (chip[:own].astype(f32) + swap(chip[own:], "xl").astype(f32)).astype(bf16)

    kv_sum = over_xl(chip_sums(normed, (grad_kv_a, grad_kv_b))[0])
    gain_sum = over_xl((gain_cols.astype(f32) + swap(gain_cols, "c").astype(f32)).astype(bf16))
    late = summed(jnp.concatenate([query_sum, out_sum, kv_sum, gain_sum], axis=1))
    mixed_out = matmul_nt(mixed, order).astype(bf16)
    late, near, far, mixed_out, tokens_grad = lax.optimization_barrier(
        (late, ffn_rows[:dp_rows], ffn_rows[dp_rows:], mixed_out, tokens_grad)
    )
    qo_share = late[:, : 2 * head_dim].reshape(dp_rows, 2, head_dim)
    x_sum = late[:, 2 * head_dim :].astype(bf16)
    x_sum = x_sum.astype(f32) + swap(x_sum, "xh").astype(f32)
    kv_mine = x_sum[:, :head_dim]
    kv_other = swap(kv_mine.astype(bf16), "c").astype(f32)
    kv_mine = kv_mine.astype(bf16).astype(f32)
    kv_total = jnp.concatenate(
        [jnp.where(c == 0, kv_mine, kv_other), jnp.where(c == 0, kv_other, kv_mine)], axis=1
    )
    norm_total = x_sum[:, head_dim : head_dim + 4]
    head_total = x_sum[:per_dp, head_dim + 4].reshape(-1, 2)

    ffn_share = near.astype(f32) + swap(far, "xl").astype(f32)
    ffn_share = ffn_share.reshape(dp_rows, 3, wide)[:, :, :ff]

    return (
        mixed_out,
        tokens_grad,
        norm_total,
        head_total,
        qo_share,
        kv_total,
        ffn_share,
    )


def solution(mesh):
    fine = Mesh(np.asarray(mesh.devices).reshape(NZ, NXL, NY, NXH, NC), ALL)
    dp, tensor = ("z", "xl", "y"), ("xh", "c")
    return jax.shard_map(
        body,
        mesh=fine,
        in_specs=(
            P(ALL, None),
            P(),
            P(),
            P(),
            P(dp, None, tensor),
            P(dp, None),
            P(dp, None, tensor),
            P(ALL, None),
        ),
        out_specs=(
            P(ALL, None),
            P(ALL, None),
            P(dp, None),
            P(dp, None),
            P(dp, None, tensor),
            P(dp, None),
            P(dp, None, tensor),
        ),
        check_vma=False,
    )
```
